256 devices in a mesh: px: 8 (over z_lo, core), py: 32 (over z_hi, x, y).
Axes of the slice: x: 4, y: 4, z: 8 (z_hi: 2, z_lo: 4; z = z_hi * 4 + z_lo), core: 2. Of those that a mesh axis runs over, the one named last changes fastest.
Arguments:
- charges: float32 [8, 32, 512], P('px', 'py'), may hold values from -4 to 4
- cells: int32 [3, 8, 32, 512], P(None, 'px', 'py'), may hold values from 0 to 383, as said below
- fractions: float32 [3, 8, 32, 512], P(None, 'px', 'py'), may hold values from 0 to 1
- filled: int32 [8, 32], P('px', 'py'), may hold values from 256 to 512, as said below
Outputs:
- potentials: float32 [8, 32, 512], P('px', 'py')
- forces: float32 [3, 8, 32, 512], P(None, 'px', 'py')
The draws below stay inside these ranges and needn't reach their ends.
Inputs may be any that keep to these rules, and one draw needn't show every extreme that they name: `cells`: component 0 lies in 0 .. 47, component 1 in 0 .. 11, component 2 in 0 .. 383. Slots at or beyond filled are padding; some brick is full in every draw.
All inputs are finite; a program needn't handle non-finite values.
Results may differ from the reference program's by a relative error of at most 0.0003.
Values sent between devices are 32-bit elements; how exact they have to be, the bound alone decides.
A program may use at most 128 MiB of HBM per device.

```python
import math
import jax
import jax.numpy as jnp
from jax import lax

GRID = 384
ORDER = 6
SLOTS = 512
BRICKS_X = 8
BRICKS_Y = 32
CX = 48
CY = 12
N_PX = 8
N_PY = 32


def draw_cells(key, part):
    key = jax.random.fold_in(key, 11)
    limits = jnp.array([CX, CY, GRID], jnp.int32).reshape(3, 1, 1, 1)
    return jax.random.randint(key, (3, BRICKS_X, BRICKS_Y, SLOTS), 0, limits, dtype=jnp.int32)


def draw_filled(key, part):
    key = jax.random.fold_in(key, 23)
    count_key, pick_key = jax.random.split(key)
    counts = jax.random.randint(count_key, (BRICKS_X * BRICKS_Y,), SLOTS // 2, SLOTS + 1, dtype=jnp.int32)
    chosen = jax.random.randint(pick_key, (), 0, BRICKS_X * BRICKS_Y, dtype=jnp.int32)
    counts = jnp.where(jnp.arange(BRICKS_X * BRICKS_Y, dtype=jnp.int32) == chosen, SLOTS, counts)
    return counts.reshape(BRICKS_X, BRICKS_Y)


def level_of(stream_key, extent, pieces, smallest, top_value):
    gain = 1.0
    for axis_at, blocks in pieces:
        draws = jax.random.uniform(jax.random.fold_in(jax.random.fold_in(stream_key, 6), axis_at), (blocks,), jnp.float32, smallest / len(pieces), top_value / len(pieces))
        gain = gain * jnp.repeat(jnp.exp(draws), extent[axis_at] // blocks).reshape((-1,) + (1,) * (len(extent) - 1 - axis_at))
    return gain


def bell_draw(rng, extent, spread, most, pieces=(), held_as=jnp.bfloat16):
    values = jax.random.normal(rng, extent, jnp.float32) * spread
    if len(pieces) > 0:
        values = level_of(rng, extent, pieces, -0.22, 0.18) * values
    return jnp.clip(values, min=-most, max=most).astype(held_as)


def setup_inputs(seed: int = 0) -> dict:
    seeds = jax.random.split(jax.random.key(seed), 5)
    return {
        "charges": bell_draw(seeds[0], (BRICKS_X, BRICKS_Y, SLOTS), 1.0, 4.0, ((0, 8), (1, 32)), jnp.float32),
        "cells": draw_cells(jax.random.fold_in(seeds[4], 71), 0),
        "fractions": jnp.clip(1.0 * jax.random.uniform(seeds[2], (3, BRICKS_X, BRICKS_Y, SLOTS), jnp.float32) ** level_of(seeds[2], (3, BRICKS_X, BRICKS_Y, SLOTS), ((1, 8), (2, 32)), -0.2, 0.2), 0.0, 1.0),
        "filled": draw_filled(jax.random.fold_in(seeds[4], 71), 0),
    }


SPLITTING = 1.6
COUPLING = 1.0 / math.pi
PRECISE = lax.Precision.HIGHEST


def spline_tables(fraction):
    values = [1.0 - fraction, fraction]
    previous = values
    for k in range(2, ORDER):
        previous = values
        zeroed = jnp.zeros_like(fraction)
        updated = []
        for j in range(k + 1):
            preceding = values[j - 1] if j >= 1 else zeroed
            current = values[j] if j < k else zeroed
            updated.append(((fraction + (k - j)) * preceding + (1.0 - fraction + j) * current) / k)
        values = updated
    zeroed = jnp.zeros_like(fraction)
    slopes = []
    for j in range(ORDER):
        preceding = previous[j - 1] if j >= 1 else zeroed
        current = previous[j] if j < ORDER - 1 else zeroed
        slopes.append(preceding - current)
    return jnp.stack(values), jnp.stack(slopes)


def stencil_tables(starts, values, slopes, length, period):
    places = lax.broadcasted_iota(jnp.int32, (length, starts.shape[0]), 0)
    weight_table = jnp.zeros((length, starts.shape[0]), jnp.float32)
    slope_table = jnp.zeros((length, starts.shape[0]), jnp.float32)
    for j in range(ORDER):
        target = starts + j
        if period > 0:
            target = target % period
        matches = places == target[None, :]
        weight_table = weight_table + jnp.where(matches, values[j][None, :], 0.0)
        slope_table = slope_table + jnp.where(matches, slopes[j][None, :], 0.0)
    return weight_table, slope_table


def brick_tables(cell_rows, fraction_rows, wide_x, wide_y):
    values, slopes = spline_tables(fraction_rows)
    margin = ORDER - 1
    table_x = stencil_tables(cell_rows[0], values[:, 0], slopes[:, 0], wide_x + margin, 0)
    table_y = stencil_tables(cell_rows[1], values[:, 1], slopes[:, 1], wide_y + margin, 0)
    table_z = stencil_tables(cell_rows[2], values[:, 2], slopes[:, 2], GRID, GRID)
    return table_x + table_y + table_z


def spread_brick(weighted, tables):
    weight_x, slope_x, weight_y, slope_y, weight_z, slope_z = tables
    columns = (weight_x * weighted[None, :])[:, None, :] * weight_y[None, :, :]
    flattened = columns.reshape(-1, columns.shape[2])
    cell_grid = lax.dot_general(flattened, weight_z, (((1,), (1,)), ((), ())), precision=PRECISE, preferred_element_type=jnp.float32)
    return cell_grid.reshape(weight_x.shape[0], weight_y.shape[0], weight_z.shape[0])


def sample_brick(grid_ext, tables, weighted):
    weight_x, slope_x, weight_y, slope_y, weight_z, slope_z = tables
    size_x = weight_x.shape[0]
    size_y = weight_y.shape[0]
    number = weight_z.shape[1]
    flattened = grid_ext.reshape(size_x * size_y, grid_ext.shape[2])
    paired = jnp.concatenate([weight_z, slope_z], axis=1)
    sampled = jnp.dot(flattened, paired, precision=PRECISE, preferred_element_type=jnp.float32)
    level = sampled[:, :number].reshape(size_x, size_y, number)
    rising = sampled[:, number:].reshape(size_x, size_y, number)
    over_y = jnp.sum(weight_y[None] * level, axis=1)
    slope_over_y = jnp.sum(slope_y[None] * level, axis=1)
    rising_over_y = jnp.sum(weight_y[None] * rising, axis=1)
    potential = jnp.sum(weight_x * over_y, axis=0)
    gradient = jnp.stack([jnp.sum(slope_x * over_y, axis=0), jnp.sum(weight_x * slope_over_y, axis=0), jnp.sum(weight_x * rising_over_y, axis=0)])
    return potential, -weighted[None, :] * gradient


def axis_terms(indices):
    signed = jnp.where(indices <= GRID // 2, indices, indices - GRID).astype(jnp.float32) / GRID
    values, slopes = spline_tables(jnp.zeros((1,), jnp.float32))
    cosine_sum = jnp.zeros(indices.shape, jnp.float32)
    sine_sum = jnp.zeros(indices.shape, jnp.float32)
    for j in range(ORDER - 1):
        angles = (2.0 * math.pi / GRID) * ((indices * j) % GRID).astype(jnp.float32)
        cosine_sum = cosine_sum + values[j, 0] * jnp.cos(angles)
        sine_sum = sine_sum + values[j, 0] * jnp.sin(angles)
    return signed * signed, 1.0 / (cosine_sum * cosine_sum + sine_sum * sine_sum)


def green(freq_x, freq_y, freq_z):
    square_x, modulus_x = axis_terms(freq_x)
    square_y, modulus_y = axis_terms(freq_y)
    square_z, modulus_z = axis_terms(freq_z)
    squared = square_x + square_y + square_z
    positive = squared > 0.0
    bounded = jnp.where(positive, squared, 1.0)
    factor = COUPLING / float(GRID * GRID * GRID)
    damping = jnp.exp(-(math.pi * math.pi / (SPLITTING * SPLITTING)) * bounded)
    return jnp.where(positive, factor * damping / bounded * modulus_x * modulus_y * modulus_z, 0.0)


def reference(charges, cells, fractions, filled):
    wide_x = GRID // N_PX
    wide_y = GRID // N_PY
    margin = ORDER - 1
    slot_count = charges.shape[2]
    occupied = (lax.broadcasted_iota(jnp.int32, charges.shape, 2) < filled[:, :, None]).astype(jnp.float32)
    weighted = (charges * occupied).reshape(N_PX * N_PY, slot_count)
    cell_rows = jnp.moveaxis(cells, 0, 2).reshape(N_PX * N_PY, 3, slot_count)
    fraction_rows = jnp.moveaxis(fractions, 0, 2).reshape(N_PX * N_PY, 3, slot_count)

    def spread_one(operands):
        charge_row, cell_row, fraction_row = operands
        return spread_brick(charge_row, brick_tables(cell_row, fraction_row, wide_x, wide_y))

    extended = lax.map(spread_one, (weighted, cell_rows, fraction_rows))
    extended = extended.reshape(N_PX, N_PY, wide_x + margin, wide_y + margin, GRID)
    folded = extended[:, :, :wide_x]
    ghost_rows = jnp.roll(extended[:, :, wide_x:], 1, axis=0)
    folded = jnp.concatenate([folded[:, :, :margin] + ghost_rows, folded[:, :, margin:]], axis=2)
    ghost_rows = jnp.roll(folded[:, :, :, wide_y:], 1, axis=1)
    folded = jnp.concatenate([folded[:, :, :, :margin] + ghost_rows, folded[:, :, :, margin:wide_y]], axis=3)
    charge_grid = folded.transpose(0, 2, 1, 3, 4).reshape(GRID, GRID, GRID)
    frequencies = jnp.arange(GRID, dtype=jnp.int32)
    multiplier = green(frequencies[:, None, None], frequencies[None, :, None], frequencies[None, None, :])
    potential_grid = jnp.real(jnp.fft.ifftn(jnp.fft.fftn(charge_grid) * multiplier)) * float(GRID * GRID * GRID)
    blocks = potential_grid.reshape(N_PX, wide_x, N_PY, wide_y, GRID).transpose(0, 2, 1, 3, 4)
    blocks = jnp.concatenate([blocks, jnp.roll(blocks, -1, axis=0)[:, :, :margin]], axis=2)
    blocks = jnp.concatenate([blocks, jnp.roll(blocks, -1, axis=1)[:, :, :, :margin]], axis=3)
    blocks = blocks.reshape(N_PX * N_PY, wide_x + margin, wide_y + margin, GRID)

    def sample_one(operands):
        grid_row, charge_row, cell_row, fraction_row = operands
        return sample_brick(grid_row, brick_tables(cell_row, fraction_row, wide_x, wide_y), charge_row)

    potentials, forces = lax.map(sample_one, (blocks, weighted, cell_rows, fraction_rows))
    potentials = (potentials * occupied.reshape(N_PX * N_PY, slot_count)).reshape(N_PX, N_PY, slot_count)
    forces = jnp.moveaxis(forces.reshape(N_PX, N_PY, 3, slot_count), 2, 0)
    return potentials, forces
```

```python
import math

import jax
import jax.numpy as jnp
import ml_dtypes
import numpy as np
from jax import lax
from jax.experimental import pallas as pl
from jax.experimental.pallas import tpu as pltpu
from jax.sharding import PartitionSpec as P

GRID = 384
ORDER = 6
SLOTS = 512
N_PX = 8
N_PY = 32
COUNT = N_PX * N_PY
WIDE_X = GRID // N_PX
WIDE_Y = GRID // N_PY
CELLS = WIDE_X * WIDE_Y
LINES = GRID // 2 + 1
HALF = 64
LANES = 128
CHUNKS = CELLS // HALF
ROWS = 208
PADDED = 256
EDGE_X = 16
EDGE_Y = 5
SPLITTING = 1.6
COUPLING = 1.0 / math.pi
MESH = pl.DeviceIdType.MESH
NT = (((1,), (1,)), ((), ()))
NN = (((1,), (0,)), ((), ()))
CLASSES = ((0, 0, WIDE_X, WIDE_Y), (0, 1, WIDE_X, EDGE_Y), (1, 0, EDGE_X, WIDE_Y), (1, 1, EDGE_X, EDGE_Y))


def halves(table):
    high = table.astype(ml_dtypes.bfloat16)
    low = (table - high.astype(np.float64)).astype(ml_dtypes.bfloat16)
    return high, low


def chunked(first, second):
    rows = first.shape[0]
    pair = np.stack([first.reshape(rows, CHUNKS, HALF), second.reshape(rows, CHUNKS, HALF)], axis=2)
    return np.ascontiguousarray(pair.reshape(rows, CHUNKS, LANES).transpose(1, 0, 2))


def turn(numerators, period):
    return 2.0 * math.pi / period * np.mod(numerators, period).astype(np.float64)


def line_table():
    at = np.arange(GRID)
    angles = turn(np.arange(LINES)[:, None] * at[None, :], GRID)
    table = np.zeros((2, PADDED, GRID))
    table[0, :LINES] = np.cos(angles)
    table[1, :LINES] = -np.sin(angles)
    return table.reshape(2 * PADDED, GRID)


def brick_table():
    device = np.arange(COUNT)
    a, b = device // N_PY, device % N_PY
    angles = turn(4 * a[:, None] * a[None, :] + b[:, None] * b[None, :], N_PY)
    return np.concatenate([np.cos(angles), -np.sin(angles)])


def twiddle_tables():
    device = np.arange(COUNT)
    cell = np.arange(CELLS)
    a, b = device // N_PY, device % N_PY
    y, x = cell // WIDE_X, cell % WIDE_X
    angles = turn(a[:, None] * x[None, :] + b[:, None] * y[None, :], GRID)
    cosines, sines = np.cos(angles), -np.sin(angles)
    return chunked(cosines, cosines), chunked(-sines, sines)


def cell_table():
    cell = np.arange(CELLS)
    y, x = cell // WIDE_X, cell % WIDE_X
    angles = turn(4 * y[:, None] * y[None, :] + x[:, None] * x[None, :], WIDE_X)
    cosines, sines = np.cos(angles), -np.sin(angles)
    table = np.zeros((CHUNKS, 2, HALF, CHUNKS, 2, HALF))
    shape = (CHUNKS, HALF, CHUNKS, HALF)
    table[:, 0, :, :, 0, :] = cosines.reshape(shape)
    table[:, 0, :, :, 1, :] = sines.reshape(shape)
    table[:, 1, :, :, 0, :] = -sines.reshape(shape)
    table[:, 1, :, :, 1, :] = cosines.reshape(shape)
    return table.reshape(2 * CELLS, 2 * CELLS)


def axis_terms(indices):
    signed = np.where(indices <= GRID // 2, indices, indices - GRID) / GRID
    values = [1.0, 0.0]
    for k in range(2, ORDER):
        values = [
            ((k - j) * (values[j - 1] if j >= 1 else 0.0) + (1.0 + j) * (values[j] if j < k else 0.0)) / k
            for j in range(k + 1)
        ]
    total = sum(values[j] * np.exp(1j * turn(indices * j, GRID)) for j in range(ORDER - 1))
    return signed * signed, 1.0 / np.abs(total) ** 2


def green_tables():
    device = np.arange(COUNT)
    cell = np.arange(CELLS)
    freq_x = (device // N_PY)[:, None] + N_PX * (cell % WIDE_X)[None, :]
    freq_y = (device % N_PY)[:, None] + N_PY * (cell // WIDE_X)[None, :]
    square_x, modulus_x = axis_terms(freq_x)
    square_y, modulus_y = axis_terms(freq_y)
    squares = square_x + square_y
    rate = math.pi * math.pi / (SPLITTING * SPLITTING)
    gains = np.exp(-rate * squares) * modulus_x * modulus_y
    square_z, modulus_z = axis_terms(np.arange(LINES))
    weight = np.full(LINES, 2.0)
    weight[0] = weight[-1] = 1.0
    factor = COUPLING / float(GRID) ** 3
    line = np.zeros((ROWS, 2, LANES))
    line[:LINES, 0] = square_z[:, None]
    line[:LINES, 1] = (factor * weight * np.exp(-rate * square_z) * modulus_z)[:, None]
    return chunked(squares, squares), chunked(gains, -gains), line.reshape(ROWS, 2 * LANES)


def split(value):
    high = value.astype(jnp.bfloat16)
    return high, (value - high.astype(jnp.float32)).astype(jnp.bfloat16)


def product(left, right, dims):
    def one(a, b):
        return lax.dot_general(a, b, dims, preferred_element_type=jnp.float32)

    return one(left[0], right[0]) + one(left[0], right[1]) + one(left[1], right[0])


def spline_rows(fraction):
    values = [1.0 - fraction, fraction]
    previous = values
    for k in range(2, ORDER):
        previous = values
        updated = []
        for j in range(k + 1):
            terms = []
            if j >= 1:
                terms.append((fraction + float(k - j)) * previous[j - 1])
            if j < k:
                terms.append((float(1 + j) - fraction) * previous[j])
            updated.append(sum(terms[1:], terms[0]) * (1.0 / k))
        values = updated
    slopes = []
    for j in range(ORDER):
        if j == 0:
            slopes.append(-previous[0])
        elif j == ORDER - 1:
            slopes.append(previous[j - 1])
        else:
            slopes.append(previous[j - 1] - previous[j])
    return values, slopes


def place(offset, rows):
    total = jnp.zeros(offset.shape, jnp.float32)
    for j in range(ORDER):
        total = jnp.where(offset == j, rows[j], total)
    return total


def swap(value):
    return pltpu.roll(value, HALF, 1)


def kernel(
    charges,
    cells,
    fractions,
    filled,
    line_hi_any,
    line_lo_any,
    brick_hi_any,
    brick_lo_any,
    cell_hi_any,
    cell_lo_any,
    twiddle_any,
    green_any,
    line_green,
    potential_out,
    force_out,
    line_hi,
    line_lo,
    brick_hi,
    brick_lo,
    cell_hi,
    cell_lo,
    twiddle,
    green,
    atoms,
    wx,
    sx,
    wy,
    sy,
    wz_hi,
    wz_lo,
    column_hi,
    column_lo,
    grid,
    outbound,
    inbound,
    multiplier,
    first_hi,
    first_lo,
    second_hi,
    second_lo,
    returning,
    returned,
    turned_hi,
    turned_lo,
    field_hi,
    field_lo,
    sampled,
    partials,
    received,
    table_sems,
    atom_send,
    atom_recv,
    out_send,
    out_recv,
    back_send,
    back_recv,
    part_send,
    part_recv,
):
    px = lax.axis_index("px")
    py = lax.axis_index("py")
    me = px * N_PY + py

    barrier = pltpu.get_barrier_semaphore()

    def greet(step, carry):
        other = lax.rem(me + step, COUNT)
        pl.semaphore_signal(barrier, inc=1, device_id=(other // N_PY, lax.rem(other, N_PY)), device_id_type=MESH)
        return carry

    lax.fori_loop(1, COUNT, greet, 0)

    tables = [
        pltpu.make_async_copy(source, target, table_sems.at[number])
        for number, (source, target) in enumerate(
            [
                (line_hi_any, line_hi),
                (line_lo_any, line_lo),
                (brick_hi_any, brick_hi),
                (brick_lo_any, brick_lo),
                (twiddle_any, twiddle),
                (green_any, green),
                (cell_hi_any, cell_hi),
                (cell_lo_any, cell_lo),
            ]
        )
    ]
    for table in tables:
        table.start()

    slot = lax.broadcasted_iota(jnp.int32, (1, SLOTS), 1)
    occupied = (slot < filled[...]).astype(jnp.float32)
    weighted = charges[0] * occupied
    atoms[0, 0:1] = weighted
    for d in range(3):
        atoms[0, 1 + d : 2 + d] = cells[d, 0].astype(jnp.float32)
        atoms[0, 4 + d : 5 + d] = fractions[d, 0]
    atoms[0, 7:8] = jnp.zeros((1, SLOTS), jnp.float32)
    returned[:, LINES - 1 :, :] = jnp.zeros((CHUNKS, PADDED - LINES + 1, LANES), jnp.float32)

    def side_tables(number):
        step_x, step_y, size_x, size_y = CLASSES[number]
        values, slopes = spline_rows(atoms[number, 4:7])
        for row, step, wide, size, weights, rises in (
            (0, step_x, WIDE_X, size_x, wx, sx),
            (1, step_y, WIDE_Y, 16, wy, sy),
        ):
            start = atoms[number, 1 + row : 2 + row].astype(jnp.int32) - step * wide
            offset = lax.broadcasted_iota(jnp.int32, (size, SLOTS), 0) - start
            weights[number, :size] = place(offset, [v[row : row + 1] for v in values])
            rises[number, :size] = place(offset, [v[row : row + 1] for v in slopes])

    def depth_tables(number, kind):
        rows = [v[2:3] for v in spline_rows(atoms[number, 4:7])[kind]]
        start = atoms[number, 3:4].astype(jnp.int32)
        lanes = pl.ds((2 * number + kind) * SLOTS, SLOTS)

        def block(step, carry):
            at = pl.multiple_of(step * 16, 16)
            offset = lax.broadcasted_iota(jnp.int32, (16, SLOTS), 0) + at - start
            offset = jnp.where(offset < 0, offset + GRID, offset)
            high, low = split(place(offset, rows))
            wz_hi[pl.ds(at, 16), lanes] = high
            wz_lo[pl.ds(at, 16), lanes] = low
            return carry

        lax.fori_loop(0, GRID // 16, block, 0)

    def spread(number):
        size_x, size_y = CLASSES[number][2:]
        charged = wx[number, :size_x] * atoms[number, 0:1]
        for k in range(size_y):
            high, low = split(charged * wy[number, k : k + 1])
            column_hi[k * size_x : (k + 1) * size_x] = high
            column_lo[k * size_x : (k + 1) * size_x] = low
        lanes = pl.ds(2 * number * SLOTS, SLOTS)
        total = size_x * size_y
        return product((column_hi[:total], column_lo[:total]), (wz_hi[:, lanes], wz_lo[:, lanes]), NT)

    side_tables(0)
    depth_tables(0, 0)

    pl.semaphore_wait(barrier, COUNT - 1)

    atom_copies = []
    for number in range(1, 4):
        step_x, step_y = CLASSES[number][:2]
        target = (lax.rem(px + step_x, N_PX), lax.rem(py + step_y, N_PY))
        copy = pltpu.make_async_remote_copy(
            atoms.at[0], atoms.at[number], atom_send.at[number], atom_recv.at[number], device_id=target, device_id_type=MESH
        )
        copy.start()
        atom_copies.append(copy)

    grid[:CELLS] = spread(0)
    grid[CELLS:] = jnp.zeros((CHUNKS * HALF + HALF - CELLS, GRID), jnp.float32)
    for number in range(1, 4):
        atom_copies[number - 1].wait_recv()
        side_tables(number)
        depth_tables(number, 0)
        size_x, size_y = CLASSES[number][2:]
        added = spread(number)
        for k in range(size_y):
            grid[k * WIDE_X : k * WIDE_X + size_x] += added[k * size_x : (k + 1) * size_x]

    tables[0].wait()
    tables[1].wait()
    dense = split(grid[...])
    cosine_part = product((line_hi[:ROWS], line_lo[:ROWS]), dense, NT)
    sine_part = product((line_hi[PADDED : PADDED + ROWS], line_lo[PADDED : PADDED + ROWS]), dense, NT)
    lower = lax.broadcasted_iota(jnp.int32, (ROWS, LANES), 1) < HALF
    for j in range(CHUNKS):
        at = (j // 2) * LANES
        cosine_block = cosine_part[:, at : at + LANES]
        sine_block = sine_part[:, at : at + LANES]
        if j % 2 == 0:
            outbound[j] = jnp.where(lower, cosine_block, swap(sine_block))
        else:
            outbound[j] = jnp.where(lower, swap(cosine_block), sine_block)

    def send_line(line, to_x, to_y):
        mine = jnp.logical_and(to_x == px, to_y == py)

        @pl.when(mine)
        def _():
            pltpu.make_async_copy(outbound.at[:, pl.ds(line, 1), :], inbound.at[:, pl.ds(me, 1), :], out_recv).start()

        @pl.when(jnp.logical_not(mine))
        def _():
            pltpu.make_async_remote_copy(
                outbound.at[:, pl.ds(line, 1), :],
                inbound.at[:, pl.ds(me, 1), :],
                out_send,
                out_recv,
                device_id=(to_x, to_y),
                device_id_type=MESH,
            ).start()

    def send_even(step, carry):
        line = lax.rem(step + me, 128)
        send_line(line, 2 * (line // N_PY), lax.rem(line, N_PY))
        return carry

    def send_odd(step, carry):
        line = lax.rem(step + me, 64)
        depth = line // 16
        pair = 2 * lax.rem(line, 16)
        send_line(128 + line, 2 * depth + 1, pair + lax.rem(depth + pair // 4, 2))
        return carry

    lax.fori_loop(0, 128, send_even, 0)
    lax.fori_loop(0, 64, send_odd, 0)
    send_line(LINES - 1, 1, 1)

    odd = lax.rem(px, 2)
    depth = px // 2
    order = depth * N_PY + py
    last = jnp.logical_and(px == 1, py == 1)
    matching = lax.rem(depth + py // 4 + py, 2) == 0
    active = jnp.logical_or(jnp.logical_or(odd == 0, last), matching)
    line_me = (1 - odd) * order + odd * (128 + order // 2)
    line_me = line_me + last.astype(jnp.int32) * (LINES - 1 - 128)

    for number in range(4):
        depth_tables(number, 1)
    for table in tables[2:]:
        table.wait()

    def wait_rows(buffer, count, semaphore):
        view = buffer.at[:, pl.ds(0, count), :]
        pltpu.make_async_copy(view, view, semaphore).wait()

    @pl.when(active)
    def _():
        scalars = line_green[pl.ds(line_me, 1), :]
        square_z = scalars[:, :LANES]
        gain_z = scalars[:, LANES:]
        for j in range(CHUNKS):
            squared = green[0, j] + square_z
            positive = squared > 0.0
            bounded = jnp.where(positive, squared, 1.0)
            multiplier[j] = jnp.where(positive, green[1, j] * gain_z / bounded, 0.0)

        wait_rows(inbound, COUNT, out_recv)
        left = lax.broadcasted_iota(jnp.int32, (COUNT, LANES), 1) < HALF
        groups = [(0, 2), (2, 4), (4, 6), (6, 8), (8, 9)]
        brick_pair = (brick_hi[...], brick_lo[...])

        def turned(value, j):
            return value * twiddle[0, j] + swap(value) * twiddle[1, j]

        for begin, end in groups:
            block = jnp.concatenate([inbound[j] for j in range(begin, end)], axis=1)
            mixed = product(brick_pair, split(block), NN)
            for j in range(begin, end):
                at = (j - begin) * LANES
                upper = mixed[:COUNT, at : at + LANES]
                crossed = swap(mixed[COUNT:, at : at + LANES])
                value = upper + jnp.where(left, -crossed, crossed)
                high, low = split(turned(value, j))
                first_hi[:, j * LANES : (j + 1) * LANES] = high
                first_lo[:, j * LANES : (j + 1) * LANES] = low
        for begin, end in groups:
            lanes = slice(begin * LANES, end * LANES)
            block = product((first_hi[...], first_lo[...]), (cell_hi[:, lanes], cell_lo[:, lanes]), NN)
            for j in range(begin, end):
                at = (j - begin) * LANES
                high, low = split(block[:, at : at + LANES] * multiplier[j])
                second_hi[:, j * LANES : (j + 1) * LANES] = high
                second_lo[:, j * LANES : (j + 1) * LANES] = low
        for begin, end in groups:
            lanes = slice(begin * LANES, end * LANES)
            block = product((second_hi[...], second_lo[...]), (cell_hi[:, lanes], cell_lo[:, lanes]), NN)
            block = jnp.concatenate(
                [turned(block[:, (j - begin) * LANES : (j - begin + 1) * LANES], j) for j in range(begin, end)], axis=1
            )
            mixed = product(brick_pair, split(block), NN)
            for j in range(begin, end):
                at = (j - begin) * LANES
                upper = mixed[:COUNT, at : at + LANES]
                crossed = swap(mixed[COUNT:, at : at + LANES])
                returning[j] = jnp.where(left, upper, -upper) - crossed

        def send_back(step, carry):
            other = lax.rem(me + step, COUNT)
            pltpu.make_async_remote_copy(
                returning.at[:, pl.ds(other, 1), :],
                returned.at[:, pl.ds(line_me, 1), :],
                back_send,
                back_recv,
                device_id=(other // N_PY, lax.rem(other, N_PY)),
                device_id_type=MESH,
            ).start()
            return carry

        pltpu.make_async_copy(returning.at[:, pl.ds(me, 1), :], returned.at[:, pl.ds(line_me, 1), :], back_recv).start()
        lax.fori_loop(1, COUNT, send_back, 0)

    wait_rows(returned, LINES, back_recv)
    for j in range(CHUNKS):
        high, low = split(returned[j].T)
        rows = slice(j * HALF, (j + 1) * HALF)
        turned_hi[rows, :PADDED] = high[:HALF]
        turned_hi[rows, PADDED:] = high[HALF:]
        turned_lo[rows, :PADDED] = low[:HALF]
        turned_lo[rows, PADDED:] = low[HALF:]
    high, low = split(product((turned_hi[...], turned_lo[...]), (line_hi[...], line_lo[...]), NN))
    field_hi[...] = high
    field_lo[...] = low

    def sample(number):
        size_x, size_y = CLASSES[number][2:]
        total = size_x * size_y
        if size_x == WIDE_X:
            field = (field_hi[:total], field_lo[:total])
        else:
            field = tuple(
                jnp.concatenate([part[k * WIDE_X : k * WIDE_X + size_x] for k in range(size_y)], axis=0)
                for part in (field_hi, field_lo)
            )
        lanes = slice(2 * number * SLOTS, 2 * (number + 1) * SLOTS)
        sampled[:total] = product(field, (wz_hi[:, lanes], wz_lo[:, lanes]), NN)

        def block(step, carry):
            at = pl.multiple_of(step * LANES, LANES)
            here = pl.ds(at, LANES)
            over_y = jnp.zeros((size_x, LANES), jnp.float32)
            slope_over_y = over_y
            rising_over_y = over_y
            for k in range(size_y):
                rows = slice(k * size_x, (k + 1) * size_x)
                level = sampled[rows, here]
                rising = sampled[rows, pl.ds(SLOTS + at, LANES)]
                weight = wy[number, k : k + 1, here]
                over_y += weight * level
                slope_over_y += sy[number, k : k + 1, here] * level
                rising_over_y += weight * rising
            weight = wx[number, :size_x, here]
            partials[number, 0:1, here] = jnp.sum(weight * over_y, axis=0, keepdims=True)
            partials[number, 1:2, here] = jnp.sum(sx[number, :size_x, here] * over_y, axis=0, keepdims=True)
            partials[number, 2:3, here] = jnp.sum(weight * slope_over_y, axis=0, keepdims=True)
            partials[number, 3:4, here] = jnp.sum(weight * rising_over_y, axis=0, keepdims=True)
            return carry

        lax.fori_loop(0, SLOTS // LANES, block, 0)

    part_copies = []
    for number in range(1, 4):
        sample(number)
        step_x, step_y = CLASSES[number][:2]
        target = (lax.rem(px + N_PX - step_x, N_PX), lax.rem(py + N_PY - step_y, N_PY))
        copy = pltpu.make_async_remote_copy(
            partials.at[number],
            received.at[number],
            part_send.at[number],
            part_recv.at[number],
            device_id=target,
            device_id_type=MESH,
        )
        copy.start()
        part_copies.append(copy)
    sample(0)
    summed = partials[0, 0:4]
    for number in range(1, 4):
        part_copies[number - 1].wait_recv()
        summed = summed + received[number, 0:4]
    potential_out[0] = summed[0:1] * occupied
    for d in range(3):
        force_out[d, 0] = -weighted * summed[1 + d : 2 + d]

    for copy in atom_copies + part_copies:
        copy.wait_send()

    @pl.when(active)
    def _():
        wait_rows(outbound, LINES - 1, out_send)
        wait_rows(returning, COUNT - 1, back_send)

    @pl.when(jnp.logical_not(active))
    def _():
        wait_rows(outbound, LINES, out_send)


def shards(charges, cells, fractions, filled):
    line = halves(line_table())
    brick = halves(brick_table())
    cell = halves(cell_table())
    twiddle = np.stack(twiddle_tables()).astype(np.float32)
    squares, gains, line_green = green_tables()
    green = np.stack([squares, gains]).astype(np.float32)
    constants = [*line, *brick, *cell, twiddle, green, line_green.astype(np.float32)]
    f32, bf16 = jnp.float32, jnp.bfloat16
    vmem = pltpu.VMEM
    message = vmem((CHUNKS, COUNT, LANES), f32)
    plane = vmem((COUNT, 2 * CELLS), bf16)
    whole = pl.BlockSpec(memory_space=pltpu.VMEM)
    distant = pl.BlockSpec(memory_space=pl.ANY)
    return pl.pallas_call(
        kernel,
        out_shape=(jax.ShapeDtypeStruct((1, 1, SLOTS), f32), jax.ShapeDtypeStruct((3, 1, 1, SLOTS), f32)),
        in_specs=[whole] * 4 + [distant] * 8 + [whole],
        out_specs=(whole, whole),
        scratch_shapes=[
            vmem((2 * PADDED, GRID), bf16),
            vmem((2 * PADDED, GRID), bf16),
            vmem((2 * COUNT, COUNT), bf16),
            vmem((2 * COUNT, COUNT), bf16),
            vmem((2 * CELLS, 2 * CELLS), bf16),
            vmem((2 * CELLS, 2 * CELLS), bf16),
            vmem((2, CHUNKS, COUNT, LANES), f32),
            vmem((2, CHUNKS, COUNT, LANES), f32),
            vmem((4, 8, SLOTS), f32),
            vmem((4, WIDE_X, SLOTS), f32),
            vmem((4, WIDE_X, SLOTS), f32),
            vmem((4, 16, SLOTS), f32),
            vmem((4, 16, SLOTS), f32),
            vmem((GRID, 8 * SLOTS), bf16),
            vmem((GRID, 8 * SLOTS), bf16),
            vmem((CELLS, SLOTS), bf16),
            vmem((CELLS, SLOTS), bf16),
            vmem((CELLS + HALF, GRID), f32),
            vmem((CHUNKS, ROWS, LANES), f32),
            message,
            message,
            plane,
            plane,
            plane,
            plane,
            message,
            message,
            vmem((CELLS, 2 * PADDED), bf16),
            vmem((CELLS, 2 * PADDED), bf16),
            vmem((CELLS, GRID), bf16),
            vmem((CELLS, GRID), bf16),
            vmem((CELLS, 2 * SLOTS), f32),
            vmem((4, 8, SLOTS), f32),
            vmem((4, 8, SLOTS), f32),
            pltpu.SemaphoreType.DMA((8,)),
            pltpu.SemaphoreType.DMA((4,)),
            pltpu.SemaphoreType.DMA((4,)),
            pltpu.SemaphoreType.DMA,
            pltpu.SemaphoreType.DMA,
            pltpu.SemaphoreType.DMA,
            pltpu.SemaphoreType.DMA,
            pltpu.SemaphoreType.DMA((4,)),
            pltpu.SemaphoreType.DMA((4,)),
        ],
        compiler_params=pltpu.CompilerParams(
            collective_id=0, has_side_effects=True, vmem_limit_bytes=56 * 1024 * 1024
        ),
    )(charges, cells, fractions, filled, *[jnp.asarray(table) for table in constants])


def solution(mesh):
    placed = (
        P("px", "py", None),
        P(None, "px", "py", None),
        P(None, "px", "py", None),
        P("px", "py"),
    )
    return jax.shard_map(
        shards,
        mesh=mesh,
        in_specs=placed,
        out_specs=(P("px", "py", None), P(None, "px", "py", None)),
        check_vma=False,
    )
```

```python
import math

import jax
import jax.numpy as jnp
import ml_dtypes
import numpy as np
from jax import lax
from jax.experimental import pallas as pl
from jax.experimental.pallas import tpu as pltpu
from jax.sharding import PartitionSpec as P

GRID = 384
ORDER = 6
SLOTS = 512
N_PX = 8
N_PY = 32
COUNT = N_PX * N_PY
WIDE_X = GRID // N_PX
WIDE_Y = GRID // N_PY
CELLS = WIDE_X * WIDE_Y
LINES = GRID // 2 + 1
HALF = 64
LANES = 128
CHUNKS = CELLS // HALF
ROWS = 208
PADDED = 256
EDGE_X = 16
EDGE_Y = 5
SPLITTING = 1.6
COUPLING = 1.0 / math.pi
MESH = pl.DeviceIdType.MESH
NT = (((1,), (1,)), ((), ()))
NN = (((1,), (0,)), ((), ()))
GROUPS = ((0, 6, 0, 8), (6, 9, 8, 12))
CLASSES = ((0, 0, WIDE_X, WIDE_Y), (0, 1, WIDE_X, EDGE_Y), (1, 0, EDGE_X, WIDE_Y), (1, 1, EDGE_X, EDGE_Y))


def halves(table):
    high = table.astype(ml_dtypes.bfloat16)
    low = (table - high.astype(np.float64)).astype(ml_dtypes.bfloat16)
    return high, low


def chunked(first, second):
    rows = first.shape[0]
    pair = np.stack([first.reshape(rows, CHUNKS, HALF), second.reshape(rows, CHUNKS, HALF)], axis=2)
    return np.ascontiguousarray(pair.reshape(rows, CHUNKS, LANES).transpose(1, 0, 2))


def turn(numerators, period):
    return 2.0 * math.pi / period * np.mod(numerators, period).astype(np.float64)


def line_table():
    at = np.arange(GRID)
    angles = turn(np.arange(LINES)[:, None] * at[None, :], GRID)
    table = np.zeros((2, PADDED, GRID))
    table[0, :LINES] = np.cos(angles)
    table[1, :LINES] = -np.sin(angles)
    return table.reshape(2 * PADDED, GRID)


def brick_table():
    device = np.arange(COUNT)
    a, b = device // N_PY, device % N_PY
    angles = turn(4 * a[:, None] * a[None, :] + b[:, None] * b[None, :], N_PY)
    return np.concatenate([np.cos(angles), -np.sin(angles)])


def twiddle_tables():
    device = np.arange(COUNT)
    cell = np.arange(CELLS)
    a, b = device // N_PY, device % N_PY
    y, x = cell // WIDE_X, cell % WIDE_X
    angles = turn(a[:, None] * x[None, :] + b[:, None] * y[None, :], GRID)
    cosines, sines = np.cos(angles), -np.sin(angles)
    return chunked(cosines, cosines), chunked(-sines, sines)


def cell_table():
    cell = np.arange(CELLS)
    y, x = cell // WIDE_X, cell % WIDE_X
    angles = turn(4 * y[:, None] * y[None, :] + x[:, None] * x[None, :], WIDE_X)
    cosines, sines = np.cos(angles), -np.sin(angles)
    table = np.zeros((CHUNKS, 2, HALF, CHUNKS, 2, HALF))
    shape = (CHUNKS, HALF, CHUNKS, HALF)
    table[:, 0, :, :, 0, :] = cosines.reshape(shape)
    table[:, 0, :, :, 1, :] = sines.reshape(shape)
    table[:, 1, :, :, 0, :] = -sines.reshape(shape)
    table[:, 1, :, :, 1, :] = cosines.reshape(shape)
    return table.reshape(2 * CELLS, 2 * CELLS)


def axis_terms(indices):
    signed = np.where(indices <= GRID // 2, indices, indices - GRID) / GRID
    values = [1.0, 0.0]
    for k in range(2, ORDER):
        values = [
            ((k - j) * (values[j - 1] if j >= 1 else 0.0) + (1.0 + j) * (values[j] if j < k else 0.0)) / k
            for j in range(k + 1)
        ]
    total = sum(values[j] * np.exp(1j * turn(indices * j, GRID)) for j in range(ORDER - 1))
    return signed * signed, 1.0 / np.abs(total) ** 2


def green_tables():
    device = np.arange(COUNT)
    cell = np.arange(CELLS)
    freq_x = (device // N_PY)[:, None] + N_PX * (cell % WIDE_X)[None, :]
    freq_y = (device % N_PY)[:, None] + N_PY * (cell // WIDE_X)[None, :]
    square_x, modulus_x = axis_terms(freq_x)
    square_y, modulus_y = axis_terms(freq_y)
    squares = square_x + square_y
    rate = math.pi * math.pi / (SPLITTING * SPLITTING)
    gains = np.exp(-rate * squares) * modulus_x * modulus_y
    square_z, modulus_z = axis_terms(np.arange(LINES))
    weight = np.full(LINES, 2.0)
    weight[0] = weight[-1] = 1.0
    factor = COUPLING / float(GRID) ** 3
    line = np.zeros((ROWS, 2, LANES))
    line[:LINES, 0] = square_z[:, None]
    line[:LINES, 1] = (factor * weight * np.exp(-rate * square_z) * modulus_z)[:, None]
    return chunked(squares, squares), chunked(gains, -gains), line.reshape(ROWS, 2 * LANES)


def split(value):
    high = value.astype(jnp.bfloat16)
    return high, (value - high.astype(jnp.float32)).astype(jnp.bfloat16)


def product(left, right, dims):
    def one(a, b):
        return lax.dot_general(a, b, dims, preferred_element_type=jnp.float32)

    rows = left[0].shape[0]
    both = one(jnp.concatenate([left[0], left[1]], axis=0), right[0])
    return both[:rows] + both[rows:] + one(left[0], right[1])


def spline_rows(fraction):
    values = [1.0 - fraction, fraction]
    previous = values
    for k in range(2, ORDER):
        previous = values
        updated = []
        for j in range(k + 1):
            terms = []
            if j >= 1:
                terms.append((fraction + float(k - j)) * previous[j - 1])
            if j < k:
                terms.append((float(1 + j) - fraction) * previous[j])
            updated.append(sum(terms[1:], terms[0]) * (1.0 / k))
        values = updated
    slopes = []
    for j in range(ORDER):
        if j == 0:
            slopes.append(-previous[0])
        elif j == ORDER - 1:
            slopes.append(previous[j - 1])
        else:
            slopes.append(previous[j - 1] - previous[j])
    return values, slopes


def place(offset, rows):
    total = jnp.zeros(offset.shape, jnp.float32)
    for j in range(ORDER):
        total = jnp.where(offset == j, rows[j], total)
    return total


def swap(value):
    return pltpu.roll(value, HALF, 1)


def kernel(
    charges,
    cells,
    fractions,
    filled,
    line_hi_any,
    line_lo_any,
    brick_hi_any,
    brick_lo_any,
    cell_hi_any,
    cell_lo_any,
    twiddle_any,
    green_any,
    line_green,
    result,
    line_hi,
    line_lo,
    brick_hi,
    brick_lo,
    cell_hi,
    cell_lo,
    twiddle,
    green,
    atoms,
    wx,
    sx,
    wy,
    sy,
    wz_hi,
    wz_lo,
    column_hi,
    column_lo,
    grid,
    outbound,
    inbound,
    multiplier,
    first_hi,
    first_lo,
    second_hi,
    second_lo,
    returning,
    returned,
    turned_hi,
    turned_lo,
    field_hi,
    field_lo,
    spectrum,
    rises_z,
    sampled,
    partials,
    received,
    table_sems,
    atom_send,
    atom_recv,
    out_send,
    out_recv,
    back_send,
    back_recv,
    part_send,
    part_recv,
    vouched,
):
    px = lax.axis_index("px")
    py = lax.axis_index("py")
    me = px * N_PY + py

    barrier = pltpu.get_barrier_semaphore()

    def greet(target):
        pl.semaphore_signal(barrier, inc=1, device_id=target, device_id_type=MESH)

    def greet_row(step, carry):
        greet((px, lax.rem(py + step, N_PY)))
        return carry

    def greet_column(step, carry):
        greet((lax.rem(px + step, N_PX), py))
        return carry

    greet((lax.rem(px + 1, N_PX), lax.rem(py + 1, N_PY)))
    greet((lax.rem(px + N_PX - 1, N_PX), lax.rem(py + N_PY - 1, N_PY)))
    lax.fori_loop(1, N_PX, greet_column, 0)
    lax.fori_loop(1, N_PY, greet_row, 0)

    tables = [
        pltpu.make_async_copy(source, target, table_sems.at[number])
        for number, (source, target) in enumerate(
            [
                (line_hi_any, line_hi),
                (line_lo_any, line_lo),
                (brick_hi_any, brick_hi),
                (brick_lo_any, brick_lo),
                (twiddle_any, twiddle),
                (green_any, green),
                (cell_hi_any, cell_hi),
                (cell_lo_any, cell_lo),
            ]
        )
    ]
    for table in tables:
        table.start()

    slot = lax.broadcasted_iota(jnp.int32, (1, SLOTS), 1)
    occupied = (slot < filled[...]).astype(jnp.float32)
    weighted = charges[0] * occupied
    atoms[0, 0:1] = weighted
    for d in range(3):
        atoms[0, 1 + d : 2 + d] = cells[d, 0].astype(jnp.float32)
        atoms[0, 4 + d : 5 + d] = fractions[d, 0]
    atoms[0, 7:8] = jnp.zeros((1, SLOTS), jnp.float32)
    returned[:, LINES - 1 :, :] = jnp.zeros((CHUNKS, PADDED - LINES + 1, LANES), jnp.float32)

    def side_tables(number):
        step_x, step_y, size_x, size_y = CLASSES[number]
        values, slopes = spline_rows(atoms[number, 4:7])
        for row, step, wide, size, weights, rises in (
            (0, step_x, WIDE_X, size_x, wx, sx),
            (1, step_y, WIDE_Y, 16, wy, sy),
        ):
            start = atoms[number, 1 + row : 2 + row].astype(jnp.int32) - step * wide
            offset = lax.broadcasted_iota(jnp.int32, (size, SLOTS), 0) - start
            weights[number, :size] = place(offset, [v[row : row + 1] for v in values])
            rises[number, :size] = place(offset, [v[row : row + 1] for v in slopes])

    def depth_block(start, rows, at, lanes):
        offset = lax.broadcasted_iota(jnp.int32, (16, SLOTS), 0) + at - start
        offset = jnp.where(offset < 0, offset + GRID, offset)
        high, low = split(place(offset, rows))
        wz_hi[pl.ds(at, 16), lanes] = high
        wz_lo[pl.ds(at, 16), lanes] = low

    def depth_tables(number):
        values, slopes = spline_rows(atoms[number, 4:7])
        rows = [v[2:3] for v in values]
        start = atoms[number, 3:4].astype(jnp.int32)
        for j in range(ORDER):
            rises_z[number, j : j + 1] = slopes[j][2:3]

        def block(step, carry):
            depth_block(start, rows, pl.multiple_of(step * 16, 16), pl.ds(2 * number * SLOTS, SLOTS))
            return carry

        lax.fori_loop(0, GRID // 16, block, 0)

    def slope_block(step):
        step = jnp.minimum(step, 4 * GRID // 32 - 1)
        number = lax.div(step, GRID // 32)
        at = lax.rem(step, GRID // 32) * 32
        rows = [rises_z[number, j : j + 1] for j in range(ORDER)]
        start = atoms[number, 3:4].astype(jnp.int32)
        lanes = pl.ds(pl.multiple_of((2 * number + 1) * SLOTS, SLOTS), SLOTS)
        for k in range(2):
            depth_block(start, rows, pl.multiple_of(at + 16 * k, 16), lanes)

    def spread(number, begin, end):
        size_x = CLASSES[number][2]
        end = min(end, CLASSES[number][3])
        charged = wx[number, :size_x] * atoms[number, 0:1]
        for k in range(begin, end):
            high, low = split(charged * wy[number, k : k + 1])
            at = (k - begin) * size_x
            column_hi[at : at + size_x] = high
            column_lo[at : at + size_x] = low
        lanes = pl.ds(2 * number * SLOTS, SLOTS)
        total = size_x * (end - begin)
        return product((column_hi[:total], column_lo[:total]), (wz_hi[:, lanes], wz_lo[:, lanes]), NT)

    pl.semaphore_wait(barrier, N_PX + N_PY)

    atom_copies = []
    for number in range(1, 4):
        step_x, step_y = CLASSES[number][:2]
        target = (lax.rem(px + step_x, N_PX), lax.rem(py + step_y, N_PY))
        copy = pltpu.make_async_remote_copy(
            atoms.at[0], atoms.at[number], atom_send.at[number], atom_recv.at[number], device_id=target, device_id_type=MESH
        )
        copy.start()
        atom_copies.append(copy)

    def vouch(step, carry):
        pl.semaphore_signal(vouched, inc=1, device_id=(lax.rem(px + step, N_PX), py), device_id_type=MESH)
        return carry

    lax.fori_loop(1, N_PX, vouch, 0)

    side_tables(0)
    depth_tables(0)

    def spread_near(number, begin, end):
        size_x = CLASSES[number][2]
        added = spread(number, begin, end)
        for k in range(begin, min(end, CLASSES[number][3])):
            at = (k - begin) * size_x
            grid[k * WIDE_X : k * WIDE_X + size_x] += added[at : at + size_x]

    def transform(begin, end):
        lanes = end - begin + (end - begin) % 2
        dense = split(grid[begin * HALF : (begin + lanes) * HALF])
        cosine_part = product((line_hi[:ROWS], line_lo[:ROWS]), dense, NT)
        sine_part = product((line_hi[PADDED : PADDED + ROWS], line_lo[PADDED : PADDED + ROWS]), dense, NT)
        lower = lax.broadcasted_iota(jnp.int32, (ROWS, LANES), 1) < HALF
        for j in range(begin, end):
            at = ((j - begin) // 2) * LANES
            cosine_block = cosine_part[:, at : at + LANES]
            sine_block = sine_part[:, at : at + LANES]
            if (j - begin) % 2 == 0:
                outbound[j] = jnp.where(lower, cosine_block, swap(sine_block))
            else:
                outbound[j] = jnp.where(lower, swap(cosine_block), sine_block)

    first, second = GROUPS
    grid[: second[2] * WIDE_X] = spread(0, *first[2:])
    grid[CELLS:] = jnp.zeros((HALF, GRID), jnp.float32)
    for number in range(1, 4):
        atom_copies[number - 1].wait_recv()
        side_tables(number)
        depth_tables(number)
        spread_near(number, *first[2:])
    tables[0].wait()
    tables[1].wait()
    transform(*first[:2])
    pl.semaphore_wait(vouched, N_PX - 1)

    core_me = lax.rem(px, 2)
    low_me = lax.div(px, 2)
    x_me = lax.rem(lax.div(py, 4), 4)
    y_me = lax.rem(py, 4)

    order = low_me * N_PY + py
    last = jnp.logical_and(px == 1, py == 1)
    matching = jnp.logical_and(core_me == 1, lax.rem(low_me + x_me + y_me, 2) == 0)
    active = jnp.logical_or(jnp.logical_or(core_me == 0, last), matching)
    line_me = (1 - core_me) * order + core_me * (128 + lax.div(order, 2))
    line_me = line_me + last.astype(jnp.int32) * (LINES - 1 - 128)

    def part(buffer, group, row):
        begin, end = GROUPS[group][:2]
        return buffer.at[pl.ds(begin, end - begin), pl.ds(row, 1), :]

    def keep_line(group):
        pltpu.make_async_copy(part(outbound, group, line_me), part(inbound, group, me), out_recv.at[group]).start()

    def send_line(group, line, to_x, to_y):
        pltpu.make_async_remote_copy(
            part(outbound, group, line),
            part(inbound, group, me),
            out_send.at[group],
            out_recv.at[group],
            device_id=(to_x, to_y),
            device_id_type=MESH,
        ).start()

    def send_even(group, step):
        line = lax.rem(order + step, 128)
        send_line(group, line, 2 * lax.div(line, N_PY), lax.rem(line, N_PY))

    def send_odd(group, step):
        pair = lax.rem(lax.div(order, 2) + step, 64)
        low = lax.div(pair, 16)
        to_y = 2 * lax.rem(pair, 16)
        send_line(group, 128 + pair, 2 * low + 1, to_y + lax.rem(low + lax.div(to_y, 4), 2))

    def send_group(group):
        pl.when(active)(lambda: keep_line(group))
        pl.when(core_me == 1)(lambda: send_even(group, 0))
        pl.when(jnp.logical_not(matching))(lambda: send_odd(group, 0))
        pl.when(jnp.logical_not(last))(lambda: send_line(group, LINES - 1, 1, 1))
        send_even(group, 1)

        def send_evens(step, carry):
            for k in range(7):
                send_even(group, 2 + 7 * step + k)
            slope_block(27 * group + step)
            return carry

        def send_odds(step, carry):
            for k in range(7):
                send_odd(group, 1 + 7 * step + k)
            slope_block(27 * group + 18 + step)
            return carry

        lax.fori_loop(0, 18, send_evens, 0)
        lax.fori_loop(0, 9, send_odds, 0)

    send_group(0)
    grid[second[2] * WIDE_X : CELLS] = spread(0, *second[2:])
    spread_near(2, *second[2:])
    transform(*second[:2])
    send_group(1)

    for table in tables[2:]:
        table.wait()

    def wait_rows(buffer, group, count, semaphores):
        begin, end = GROUPS[group][:2]
        view = buffer.at[pl.ds(begin, end - begin), pl.ds(0, count), :]
        pltpu.make_async_copy(view, view, semaphores.at[group]).wait()

    @pl.when(active)
    def _():
        left = lax.broadcasted_iota(jnp.int32, (COUNT, LANES), 1) < HALF
        brick_pair = (brick_hi[...], brick_lo[...])

        def pairs(group):
            begin, end = GROUPS[group][:2]
            return [(j, min(j + 2, end)) for j in range(begin, end, 2)]

        def turned(value, j):
            return value * twiddle[0, j] + swap(value) * twiddle[1, j]

        def gather(group):
            for begin, end in pairs(group):
                block = jnp.concatenate([inbound[j] for j in range(begin, end)], axis=1)
                mixed = product(brick_pair, split(block), NN)
                for j in range(begin, end):
                    at = (j - begin) * LANES
                    upper = mixed[:COUNT, at : at + LANES]
                    crossed = swap(mixed[COUNT:, at : at + LANES])
                    value = upper + jnp.where(left, -crossed, crossed)
                    high, low = split(turned(value, j))
                    first_hi[:, j * LANES : (j + 1) * LANES] = high
                    first_lo[:, j * LANES : (j + 1) * LANES] = low

        def over_cells(group, lanes):
            rows = slice(GROUPS[group][0] * LANES, GROUPS[group][1] * LANES)
            return product((first_hi[:, rows], first_lo[:, rows]), (cell_hi[rows, lanes], cell_lo[rows, lanes]), NN)

        every = pairs(0) + pairs(1)
        wait_rows(inbound, 0, COUNT, out_recv)
        gather(0)
        for begin, end in every:
            lanes = slice(begin * LANES, end * LANES)
            spectrum[:, lanes] = over_cells(0, lanes)

        scalars = line_green[pl.ds(line_me, 1), :]
        square_z = scalars[:, :LANES]
        gain_z = scalars[:, LANES:]
        for j in range(CHUNKS):
            squared = green[0, j] + square_z
            positive = squared > 0.0
            bounded = jnp.where(positive, squared, 1.0)
            multiplier[j] = jnp.where(positive, green[1, j] * gain_z / bounded, 0.0)

        wait_rows(inbound, 1, COUNT, out_recv)
        gather(1)
        for begin, end in every:
            lanes = slice(begin * LANES, end * LANES)
            block = spectrum[:, lanes] + over_cells(1, lanes)
            for j in range(begin, end):
                at = (j - begin) * LANES
                high, low = split(block[:, at : at + LANES] * multiplier[j])
                second_hi[:, j * LANES : (j + 1) * LANES] = high
                second_lo[:, j * LANES : (j + 1) * LANES] = low

        def send_row(group, other):
            pltpu.make_async_remote_copy(
                part(returning, group, other),
                part(returned, group, line_me),
                back_send.at[group],
                back_recv.at[group],
                device_id=(lax.div(other, N_PY), lax.rem(other, N_PY)),
                device_id_type=MESH,
            ).start()

        for group in range(2):
            for begin, end in pairs(group):
                lanes = slice(begin * LANES, end * LANES)
                block = product((second_hi[...], second_lo[...]), (cell_hi[:, lanes], cell_lo[:, lanes]), NN)
                block = jnp.concatenate(
                    [turned(block[:, (j - begin) * LANES : (j - begin + 1) * LANES], j) for j in range(begin, end)], axis=1
                )
                mixed = product(brick_pair, split(block), NN)
                for j in range(begin, end):
                    at = (j - begin) * LANES
                    upper = mixed[:COUNT, at : at + LANES]
                    crossed = swap(mixed[COUNT:, at : at + LANES])
                    returning[j] = jnp.where(left, upper, -upper) - crossed

            def send_back(step, carry, group=group):
                for k in range(5):
                    send_row(group, lax.rem(me + 1 + 5 * step + k, COUNT))
                return carry

            pltpu.make_async_copy(part(returning, group, me), part(returned, group, line_me), back_recv.at[group]).start()
            lax.fori_loop(0, (COUNT - 1) // 5, send_back, 0)

    def restore(group):
        begin, end = GROUPS[group][:2]
        wait_rows(returned, group, LINES, back_recv)
        for j in range(begin, end):
            high, low = split(returned[j].T)
            rows = slice(j * HALF, (j + 1) * HALF)
            turned_hi[rows, :PADDED] = high[:HALF]
            turned_hi[rows, PADDED:] = high[HALF:]
            turned_lo[rows, :PADDED] = low[:HALF]
            turned_lo[rows, PADDED:] = low[HALF:]
        rows = slice(begin * HALF, end * HALF)
        high, low = split(product((turned_hi[rows], turned_lo[rows]), (line_hi[...], line_lo[...]), NN))
        field_hi[rows] = high
        field_lo[rows] = low

    def sample(number, begin, end):
        size_x = CLASSES[number][2]
        end = min(end, CLASSES[number][3])
        total = size_x * (end - begin)
        if size_x == WIDE_X:
            rows = slice(begin * WIDE_X, end * WIDE_X)
            field = (field_hi[rows], field_lo[rows])
        else:
            field = tuple(
                jnp.concatenate([values[k * WIDE_X : k * WIDE_X + size_x] for k in range(begin, end)], axis=0)
                for values in (field_hi, field_lo)
            )
        lanes = slice(2 * number * SLOTS, 2 * (number + 1) * SLOTS)
        sampled[:total] = product(field, (wz_hi[:, lanes], wz_lo[:, lanes]), NN)

        def block(step, carry):
            at = pl.multiple_of(step * LANES, LANES)
            here = pl.ds(at, LANES)
            over_y = jnp.zeros((size_x, LANES), jnp.float32)
            slope_over_y = over_y
            rising_over_y = over_y
            for k in range(begin, end):
                rows = slice((k - begin) * size_x, (k - begin + 1) * size_x)
                level = sampled[rows, here]
                rising = sampled[rows, pl.ds(SLOTS + at, LANES)]
                weight = wy[number, k : k + 1, here]
                over_y += weight * level
                slope_over_y += sy[number, k : k + 1, here] * level
                rising_over_y += weight * rising
            weight = wx[number, :size_x, here]
            sums = [weight * over_y, sx[number, :size_x, here] * over_y, weight * slope_over_y, weight * rising_over_y]
            for row, values in enumerate(sums):
                total_row = jnp.sum(values, axis=0, keepdims=True)
                if begin > 0:
                    total_row = total_row + partials[number, row : row + 1, here]
                partials[number, row : row + 1, here] = total_row
            return carry

        lax.fori_loop(0, SLOTS // LANES, block, 0)

    part_copies = []

    def give(number):
        step_x, step_y = CLASSES[number][:2]
        target = (lax.rem(px + N_PX - step_x, N_PX), lax.rem(py + N_PY - step_y, N_PY))
        copy = pltpu.make_async_remote_copy(
            partials.at[number],
            received.at[number],
            part_send.at[number],
            part_recv.at[number],
            device_id=target,
            device_id_type=MESH,
        )
        copy.start()
        part_copies.append(copy)

    restore(0)
    for number in (1, 3):
        sample(number, *first[2:])
        give(number)
    sample(2, *first[2:])
    sample(0, *first[2:])
    restore(1)
    sample(2, *second[2:])
    give(2)
    sample(0, *second[2:])
    summed = partials[0, 0:4]
    for copy in part_copies:
        copy.wait_recv()
    for number in range(1, 4):
        summed = summed + received[number, 0:4]
    result[0, 0] = summed[0:1] * occupied
    for d in range(3):
        result[1 + d, 0] = -weighted * summed[1 + d : 2 + d]

    for copy in atom_copies + part_copies:
        copy.wait_send()

    @pl.when(active)
    def _():
        for group in range(2):
            wait_rows(outbound, group, LINES - 1, out_send)
            wait_rows(returning, group, COUNT - 1, back_send)

    @pl.when(jnp.logical_not(active))
    def _():
        for group in range(2):
            wait_rows(outbound, group, LINES, out_send)


def shards(charges, cells, fractions, filled):
    line = halves(line_table())
    brick = halves(brick_table())
    cell = halves(cell_table())
    twiddle = np.stack(twiddle_tables()).astype(np.float32)
    squares, gains, line_green = green_tables()
    green = np.stack([squares, gains]).astype(np.float32)
    constants = [*line, *brick, *cell, twiddle, green, line_green.astype(np.float32)]
    f32, bf16 = jnp.float32, jnp.bfloat16
    vmem = pltpu.VMEM
    message = vmem((CHUNKS, COUNT, LANES), f32)
    plane = vmem((COUNT, 2 * CELLS), bf16)
    whole = pl.BlockSpec(memory_space=pltpu.VMEM)
    distant = pl.BlockSpec(memory_space=pl.ANY)
    result = pl.pallas_call(
        kernel,
        out_shape=jax.ShapeDtypeStruct((4, 1, 1, SLOTS), f32),
        in_specs=[whole] * 4 + [distant] * 8 + [whole],
        out_specs=whole,
        scratch_shapes=[
            vmem((2 * PADDED, GRID), bf16),
            vmem((2 * PADDED, GRID), bf16),
            vmem((2 * COUNT, COUNT), bf16),
            vmem((2 * COUNT, COUNT), bf16),
            vmem((2 * CELLS, 2 * CELLS), bf16),
            vmem((2 * CELLS, 2 * CELLS), bf16),
            vmem((2, CHUNKS, COUNT, LANES), f32),
            vmem((2, CHUNKS, COUNT, LANES), f32),
            vmem((4, 8, SLOTS), f32),
            vmem((4, WIDE_X, SLOTS), f32),
            vmem((4, WIDE_X, SLOTS), f32),
            vmem((4, 16, SLOTS), f32),
            vmem((4, 16, SLOTS), f32),
            vmem((GRID, 8 * SLOTS), bf16),
            vmem((GRID, 8 * SLOTS), bf16),
            vmem((CELLS, SLOTS), bf16),
            vmem((CELLS, SLOTS), bf16),
            vmem((CELLS + HALF, GRID), f32),
            vmem((CHUNKS, ROWS, LANES), f32),
            message,
            message,
            plane,
            plane,
            plane,
            plane,
            message,
            message,
            vmem((CELLS, 2 * PADDED), bf16),
            vmem((CELLS, 2 * PADDED), bf16),
            vmem((CELLS, GRID), bf16),
            vmem((CELLS, GRID), bf16),
            vmem((COUNT, 2 * CELLS), f32),
            vmem((4, 8, SLOTS), f32),
            vmem((CELLS, 2 * SLOTS), f32),
            vmem((4, 8, SLOTS), f32),
            vmem((4, 8, SLOTS), f32),
            pltpu.SemaphoreType.DMA((8,)),
            pltpu.SemaphoreType.DMA((4,)),
            pltpu.SemaphoreType.DMA((4,)),
            pltpu.SemaphoreType.DMA((2,)),
            pltpu.SemaphoreType.DMA((2,)),
            pltpu.SemaphoreType.DMA((2,)),
            pltpu.SemaphoreType.DMA((2,)),
            pltpu.SemaphoreType.DMA((4,)),
            pltpu.SemaphoreType.DMA((4,)),
            pltpu.SemaphoreType.REGULAR,
        ],
        compiler_params=pltpu.CompilerParams(
            collective_id=0, has_side_effects=True, vmem_limit_bytes=56 * 1024 * 1024
        ),
    )(charges, cells, fractions, filled, *[jnp.asarray(table) for table in constants])
    return result[0], result[1:]


def solution(mesh):
    placed = (
        P("px", "py", None),
        P(None, "px", "py", None),
        P(None, "px", "py", None),
        P("px", "py"),
    )
    return jax.shard_map(
        shards,
        mesh=mesh,
        in_specs=placed,
        out_specs=(P("px", "py", None), P(None, "px", "py", None)),
        check_vma=False,
    )
```

```python
import math

import jax
import jax.numpy as jnp
import ml_dtypes
import numpy as np
from jax import lax
from jax.experimental import pallas as pl
from jax.experimental.pallas import tpu as pltpu
from jax.sharding import PartitionSpec as P

GRID = 384
ORDER = 6
SLOTS = 512
N_PX = 8
N_PY = 32
COUNT = N_PX * N_PY
WIDE_X = GRID // N_PX
WIDE_Y = GRID // N_PY
CELLS = WIDE_X * WIDE_Y
LINES = GRID // 2 + 1
HALF = 64
LANES = 128
CHUNKS = CELLS // HALF
ROWS = 208
PADDED = 256
EDGE_X = 16
EDGE_Y = 5
SPLITTING = 1.6
COUPLING = 1.0 / math.pi
MESH = pl.DeviceIdType.MESH
NT = (((1,), (1,)), ((), ()))
NN = (((1,), (0,)), ((), ()))
GROUPS = ((0, 6), (6, 9))
FULL_Y = 6
RUNS = (
    [((y, 0, WIDE_X), y * WIDE_X) for y in range(FULL_Y)]
    + [((y, 0, EDGE_X), FULL_Y * WIDE_X + (y - FULL_Y) * EDGE_X) for y in range(FULL_Y, WIDE_Y)]
    + [((y, EDGE_X, WIDE_X), 2 * CELLS // 3 + (y - FULL_Y) * (WIDE_X - EDGE_X)) for y in range(FULL_Y, WIDE_Y)]
)
CELL_Y = np.concatenate([np.full(end - begin, y) for (y, begin, end), _ in RUNS])
CELL_X = np.concatenate([np.arange(begin, end) for (_, begin, end), _ in RUNS])
CLASSES = ((0, 0, WIDE_X, WIDE_Y), (0, 1, WIDE_X, EDGE_Y), (1, 0, EDGE_X, WIDE_Y), (1, 1, EDGE_X, EDGE_Y))


def halves(table):
    high = table.astype(ml_dtypes.bfloat16)
    low = (table - high.astype(np.float64)).astype(ml_dtypes.bfloat16)
    return high, low


def chunked(first, second):
    rows = first.shape[0]
    pair = np.stack([first.reshape(rows, CHUNKS, HALF), second.reshape(rows, CHUNKS, HALF)], axis=2)
    return np.ascontiguousarray(pair.reshape(rows, CHUNKS, LANES).transpose(1, 0, 2))


def turn(numerators, period):
    return 2.0 * math.pi / period * np.mod(numerators, period).astype(np.float64)


def line_table():
    at = np.arange(GRID)
    angles = turn(np.arange(LINES)[:, None] * at[None, :], GRID)
    table = np.zeros((2, PADDED, GRID))
    table[0, :LINES] = np.cos(angles)
    table[1, :LINES] = -np.sin(angles)
    return table.reshape(2 * PADDED, GRID)


def brick_table():
    device = np.arange(COUNT)
    a, b = device // N_PY, device % N_PY
    angles = turn(4 * a[:, None] * a[None, :] + b[:, None] * b[None, :], N_PY)
    return np.concatenate([np.cos(angles), -np.sin(angles)])


def twiddle_tables():
    device = np.arange(COUNT)
    a, b = device // N_PY, device % N_PY
    y, x = CELL_Y, CELL_X
    angles = turn(a[:, None] * x[None, :] + b[:, None] * y[None, :], GRID)
    cosines, sines = np.cos(angles), -np.sin(angles)
    return chunked(cosines, cosines), chunked(-sines, sines)


def cell_table():
    y, x = CELL_Y, CELL_X
    angles = turn(4 * y[:, None] * y[None, :] + x[:, None] * x[None, :], WIDE_X)
    cosines, sines = np.cos(angles), -np.sin(angles)
    table = np.zeros((CHUNKS, 2, HALF, CHUNKS, 2, HALF))
    shape = (CHUNKS, HALF, CHUNKS, HALF)
    table[:, 0, :, :, 0, :] = cosines.reshape(shape)
    table[:, 0, :, :, 1, :] = sines.reshape(shape)
    table[:, 1, :, :, 0, :] = -sines.reshape(shape)
    table[:, 1, :, :, 1, :] = cosines.reshape(shape)
    return table.reshape(2 * CELLS, 2 * CELLS)


def axis_terms(indices):
    signed = np.where(indices <= GRID // 2, indices, indices - GRID) / GRID
    values = [1.0, 0.0]
    for k in range(2, ORDER):
        values = [
            ((k - j) * (values[j - 1] if j >= 1 else 0.0) + (1.0 + j) * (values[j] if j < k else 0.0)) / k
            for j in range(k + 1)
        ]
    total = sum(values[j] * np.exp(1j * turn(indices * j, GRID)) for j in range(ORDER - 1))
    return signed * signed, 1.0 / np.abs(total) ** 2


def green_tables():
    device = np.arange(COUNT)
    freq_x = (device // N_PY)[:, None] + N_PX * CELL_X[None, :]
    freq_y = (device % N_PY)[:, None] + N_PY * CELL_Y[None, :]
    square_x, modulus_x = axis_terms(freq_x)
    square_y, modulus_y = axis_terms(freq_y)
    squares = square_x + square_y
    rate = math.pi * math.pi / (SPLITTING * SPLITTING)
    gains = np.exp(-rate * squares) * modulus_x * modulus_y
    square_z, modulus_z = axis_terms(np.arange(LINES))
    weight = np.full(LINES, 2.0)
    weight[0] = weight[-1] = 1.0
    factor = COUPLING / float(GRID) ** 3
    line = np.zeros((ROWS, 2, LANES))
    line[:LINES, 0] = square_z[:, None]
    line[:LINES, 1] = (factor * weight * np.exp(-rate * square_z) * modulus_z)[:, None]
    return chunked(squares, squares), chunked(gains, -gains), line.reshape(ROWS, 2 * LANES)


def split(value):
    high = value.astype(jnp.bfloat16)
    return high, (value - high.astype(jnp.float32)).astype(jnp.bfloat16)


def product(left, right, dims):
    def one(a, b):
        return lax.dot_general(a, b, dims, preferred_element_type=jnp.float32)

    rows = left[0].shape[0]
    both = one(jnp.concatenate([left[0], left[1]], axis=0), right[0])
    return both[:rows] + both[rows:] + one(left[0], right[1])


def spline_rows(fraction):
    values = [1.0 - fraction, fraction]
    previous = values
    for k in range(2, ORDER):
        previous = values
        updated = []
        for j in range(k + 1):
            terms = []
            if j >= 1:
                terms.append((fraction + float(k - j)) * previous[j - 1])
            if j < k:
                terms.append((float(1 + j) - fraction) * previous[j])
            updated.append(sum(terms[1:], terms[0]) * (1.0 / k))
        values = updated
    slopes = []
    for j in range(ORDER):
        if j == 0:
            slopes.append(-previous[0])
        elif j == ORDER - 1:
            slopes.append(previous[j - 1])
        else:
            slopes.append(previous[j - 1] - previous[j])
    return values, slopes


def place(offset, rows):
    total = jnp.zeros(offset.shape, jnp.float32)
    for j in range(ORDER):
        total = jnp.where(offset == j, rows[j], total)
    return total


def runs_of(number, second):
    size_x, size_y = CLASSES[number][2:]
    found = []
    for (y, begin, end), at in RUNS:
        if (at >= 2 * CELLS // 3) == second and y < size_y and begin < size_x:
            found.append((y, begin, min(end, size_x), at))
    return found


def swap(value):
    return pltpu.roll(value, HALF, 1)


def hand_over(result, potentials, forces):
    potentials[...] = result[0]
    forces[...] = result[1:4]


def kernel(
    charges_any,
    cells_any,
    fractions_any,
    filled,
    line_hi_any,
    line_lo_any,
    brick_hi_any,
    brick_lo_any,
    cell_hi_any,
    cell_lo_any,
    twiddle_any,
    green_any,
    line_green_any,
    result,
    charges,
    cells,
    fractions,
    line_green,
    line_hi,
    line_lo,
    brick_hi,
    brick_lo,
    cell_hi,
    cell_lo,
    twiddle,
    green,
    atoms,
    wx,
    sx,
    wy,
    sy,
    wz_hi,
    wz_lo,
    column_hi,
    column_lo,
    grid,
    outbound,
    inbound,
    multiplier,
    first_hi,
    first_lo,
    second_hi,
    second_lo,
    returning,
    returned,
    turned_hi,
    turned_lo,
    field_hi,
    field_lo,
    spectrum,
    taps_hi,
    taps_lo,
    offsets,
    sampled,
    partials,
    received,
    table_sems,
    atom_send,
    atom_recv,
    out_send,
    out_recv,
    back_send,
    back_recv,
    part_send,
    part_recv,
    vouched,
):
    px = lax.axis_index("px")
    py = lax.axis_index("py")
    me = px * N_PY + py

    arguments = [
        pltpu.make_async_copy(source, target, table_sems.at[9 + number])
        for number, (source, target) in enumerate(
            [(charges_any, charges), (cells_any, cells), (fractions_any, fractions)]
        )
    ]
    for copy in arguments:
        copy.start()

    barrier = pltpu.get_barrier_semaphore()

    def greet(target):
        pl.semaphore_signal(barrier, inc=1, device_id=target, device_id_type=MESH)

    def greet_row(step, carry):
        greet((px, lax.rem(py + step, N_PY)))
        return carry

    def greet_column(step, carry):
        greet((lax.rem(px + step, N_PX), py))
        return carry

    greet((lax.rem(px + 1, N_PX), lax.rem(py + 1, N_PY)))
    greet((lax.rem(px + N_PX - 1, N_PX), lax.rem(py + N_PY - 1, N_PY)))
    lax.fori_loop(1, N_PX, greet_column, 0)
    lax.fori_loop(1, N_PY, greet_row, 0)

    tables = [
        pltpu.make_async_copy(source, target, table_sems.at[number])
        for number, (source, target) in enumerate(
            [
                (line_hi_any, line_hi),
                (line_lo_any, line_lo),
                (brick_hi_any, brick_hi),
                (brick_lo_any, brick_lo),
                (twiddle_any, twiddle),
                (green_any, green),
                (cell_hi_any, cell_hi),
                (cell_lo_any, cell_lo),
                (line_green_any, line_green),
            ]
        )
    ]
    for table in tables:
        table.start()
    for copy in arguments:
        copy.wait()

    slot = lax.broadcasted_iota(jnp.int32, (1, SLOTS), 1)
    occupied = (slot < filled[...]).astype(jnp.float32)
    weighted = charges[0] * occupied
    atoms[0, 0:1] = weighted
    for d in range(3):
        atoms[0, 1 + d : 2 + d] = cells[d, 0].astype(jnp.float32)
        atoms[0, 4 + d : 5 + d] = fractions[d, 0]
    atoms[0, 7:8] = jnp.zeros((1, SLOTS), jnp.float32)
    returned[:, LINES - 1 :, :] = jnp.zeros((CHUNKS, PADDED - LINES + 1, LANES), jnp.float32)

    def side_tables(number):
        step_x, step_y, size_x, size_y = CLASSES[number]
        values, slopes = spline_rows(atoms[number, 4:7])
        depth_rows(number, values, slopes)
        for row, step, wide, size, weights, rises in (
            (0, step_x, WIDE_X, size_x, wx, sx),
            (1, step_y, WIDE_Y, 16, wy, sy),
        ):
            start = atoms[number, 1 + row : 2 + row].astype(jnp.int32) - step * wide
            offset = lax.broadcasted_iota(jnp.int32, (size, SLOTS), 0) - start
            weights[number, :size] = place(offset, [v[row : row + 1] for v in values])
            rises[number, :size] = place(offset, [v[row : row + 1] for v in slopes])

    def depth_rows(number, values, slopes):
        for kind, rows in enumerate((values, slopes)):
            for j in range(ORDER):
                high, low = split(jnp.broadcast_to(rows[j][2:3], (16, SLOTS)))
                taps_hi[number, kind, j] = high
                taps_lo[number, kind, j] = low
        start = atoms[number, 3:4].astype(jnp.int32)
        offsets[number] = (lax.broadcasted_iota(jnp.int32, (16, SLOTS), 0) - start).astype(jnp.int16)

    def depth_block(number, kind, at, lanes):
        offset = offsets[number] + jnp.full((16, SLOTS), at, jnp.int32).astype(jnp.int16)
        offset = jnp.where(offset < 0, offset + jnp.int16(GRID), offset)
        high = jnp.zeros((16, SLOTS), jnp.bfloat16)
        low = high
        for j in range(ORDER):
            here = offset == j
            high = jnp.where(here, taps_hi[number, kind, j], high)
            low = jnp.where(here, taps_lo[number, kind, j], low)
        wz_hi[pl.ds(at, 16), lanes] = high
        wz_lo[pl.ds(at, 16), lanes] = low

    def depth_tables(number):
        def block(step, carry):
            depth_block(number, 0, pl.multiple_of(step * 16, 16), pl.ds(2 * number * SLOTS, SLOTS))
            return carry

        lax.fori_loop(0, GRID // 16, block, 0)

    def slope_block(step):
        step = jnp.minimum(step, 4 * GRID // 32 - 1)
        number = lax.div(step, GRID // 32)
        at = lax.rem(step, GRID // 32) * 32
        lanes = pl.ds(pl.multiple_of((2 * number + 1) * SLOTS, SLOTS), SLOTS)
        for k in range(2):
            depth_block(number, 1, pl.multiple_of(at + 16 * k, 16), lanes)

    def spread(number, second):
        charge = atoms[number, 0:1]
        total = 0
        for y, begin, end, _ in runs_of(number, second):
            high, low = split((wx[number, begin:end] * charge) * wy[number, y : y + 1])
            column_hi[total : total + end - begin] = high
            column_lo[total : total + end - begin] = low
            total += end - begin
        lanes = pl.ds(2 * number * SLOTS, SLOTS)
        return product((column_hi[:total], column_lo[:total]), (wz_hi[:, lanes], wz_lo[:, lanes]), NT)

    pl.semaphore_wait(barrier, N_PX + N_PY)

    atom_copies = []
    for number in range(1, 4):
        step_x, step_y = CLASSES[number][:2]
        target = (lax.rem(px + step_x, N_PX), lax.rem(py + step_y, N_PY))
        copy = pltpu.make_async_remote_copy(
            atoms.at[0], atoms.at[number], atom_send.at[number], atom_recv.at[number], device_id=target, device_id_type=MESH
        )
        copy.start()
        atom_copies.append(copy)

    def vouch(step, carry):
        pl.semaphore_signal(vouched, inc=1, device_id=(lax.rem(px + step, N_PX), py), device_id_type=MESH)
        return carry

    lax.fori_loop(1, N_PX, vouch, 0)

    side_tables(0)
    depth_tables(0)

    def spread_near(number):
        added = spread(number, False)
        place_at = 0
        for _, begin, end, at in runs_of(number, False):
            grid[at : at + end - begin] += added[place_at : place_at + end - begin]
            place_at += end - begin

    def transform(begin, end):
        lanes = end - begin + (end - begin) % 2
        dense = split(grid[begin * HALF : (begin + lanes) * HALF])
        cosine_part = product((line_hi[:ROWS], line_lo[:ROWS]), dense, NT)
        sine_part = product((line_hi[PADDED : PADDED + ROWS], line_lo[PADDED : PADDED + ROWS]), dense, NT)
        lower = lax.broadcasted_iota(jnp.int32, (ROWS, LANES), 1) < HALF
        for j in range(begin, end):
            at = ((j - begin) // 2) * LANES
            cosine_block = cosine_part[:, at : at + LANES]
            sine_block = sine_part[:, at : at + LANES]
            if (j - begin) % 2 == 0:
                outbound[j] = jnp.where(lower, cosine_block, swap(sine_block))
            else:
                outbound[j] = jnp.where(lower, swap(cosine_block), sine_block)

    first, second = GROUPS
    grid[: first[1] * HALF] = spread(0, False)
    grid[CELLS:] = jnp.zeros((HALF, GRID), jnp.float32)
    for number in range(1, 4):
        atom_copies[number - 1].wait_recv()
        side_tables(number)
        depth_tables(number)
        spread_near(number)
    tables[0].wait()
    tables[1].wait()
    transform(*first)
    pl.semaphore_wait(vouched, N_PX - 1)

    core_me = lax.rem(px, 2)
    low_me = lax.div(px, 2)
    x_me = lax.rem(lax.div(py, 4), 4)
    y_me = lax.rem(py, 4)

    def main_core(low, to_y):
        return lax.rem(low + lax.div(to_y, 8) + lax.div(lax.rem(to_y, 4), 2), 2)

    order = low_me * N_PY + py
    main_me = main_core(low_me, py)
    other_me = lax.rem(core_me + main_me, 2)
    last = jnp.logical_and(px == 1, py == 1)
    matching = jnp.logical_and(other_me == 1, lax.rem(low_me + x_me + y_me, 2) == 0)
    active = jnp.logical_or(jnp.logical_or(other_me == 0, last), matching)
    line_me = (1 - other_me) * order + other_me * (128 + lax.div(order, 2))
    line_me = line_me + last.astype(jnp.int32) * (LINES - 1 - 128)

    def part(buffer, group, row):
        begin, end = GROUPS[group][:2]
        return buffer.at[pl.ds(begin, end - begin), pl.ds(row, 1), :]

    def keep_line(group):
        pltpu.make_async_copy(part(outbound, group, line_me), part(inbound, group, me), out_recv.at[group]).start()

    def send_line(group, line, to_x, to_y):
        pltpu.make_async_remote_copy(
            part(outbound, group, line),
            part(inbound, group, me),
            out_send.at[group],
            out_recv.at[group],
            device_id=(to_x, to_y),
            device_id_type=MESH,
        ).start()

    def send_even(group, step):
        line = lax.rem(order + step, 128)
        low, to_y = lax.div(line, N_PY), lax.rem(line, N_PY)
        send_line(group, line, 2 * low + main_core(low, to_y), to_y)

    def send_odd(group, step):
        pair = lax.rem(lax.div(order, 2) + step, 64)
        low = lax.div(pair, 16)
        to_y = 2 * lax.rem(pair, 16)
        to_y = to_y + lax.rem(low + lax.div(to_y, 4), 2)
        send_line(group, 128 + pair, 2 * low + 1 - main_core(low, to_y), to_y)

    def send_group(group):
        pl.when(active)(lambda: keep_line(group))
        pl.when(other_me == 1)(lambda: send_even(group, 0))
        pl.when(jnp.logical_not(matching))(lambda: send_odd(group, 0))
        pl.when(jnp.logical_not(last))(lambda: send_line(group, LINES - 1, 1, 1))
        send_even(group, 1)

        def send_evens(step, carry):
            for k in range(7):
                send_even(group, 2 + 7 * step + k)
            slope_block(27 * group + step)
            return carry

        def send_odds(step, carry):
            for k in range(7):
                send_odd(group, 1 + 7 * step + k)
            slope_block(27 * group + 18 + step)
            return carry

        lax.fori_loop(0, 18, send_evens, 0)
        lax.fori_loop(0, 9, send_odds, 0)

    send_group(0)
    grid[second[0] * HALF : CELLS] = spread(0, True)
    transform(*second)
    send_group(1)

    for table in tables[2:]:
        table.wait()

    def wait_rows(buffer, group, count, semaphores):
        begin, end = GROUPS[group][:2]
        view = buffer.at[pl.ds(begin, end - begin), pl.ds(0, count), :]
        pltpu.make_async_copy(view, view, semaphores.at[group]).wait()

    @pl.when(active)
    def _():
        left = lax.broadcasted_iota(jnp.int32, (COUNT, LANES), 1) < HALF
        brick_pair = (brick_hi[...], brick_lo[...])

        def pairs(group):
            begin, end = GROUPS[group][:2]
            return [(j, min(j + 2, end)) for j in range(begin, end, 2)]

        def turned(value, j):
            return value * twiddle[0, j] + swap(value) * twiddle[1, j]

        def gather(group):
            for begin, end in pairs(group):
                block = jnp.concatenate([inbound[j] for j in range(begin, end)], axis=1)
                mixed = product(brick_pair, split(block), NN)
                for j in range(begin, end):
                    at = (j - begin) * LANES
                    upper = mixed[:COUNT, at : at + LANES]
                    crossed = swap(mixed[COUNT:, at : at + LANES])
                    value = upper + jnp.where(left, -crossed, crossed)
                    high, low = split(turned(value, j))
                    first_hi[:, j * LANES : (j + 1) * LANES] = high
                    first_lo[:, j * LANES : (j + 1) * LANES] = low

        def over_cells(group, lanes):
            rows = slice(GROUPS[group][0] * LANES, GROUPS[group][1] * LANES)
            return product((first_hi[:, rows], first_lo[:, rows]), (cell_hi[rows, lanes], cell_lo[rows, lanes]), NN)

        every = pairs(0) + pairs(1)
        wait_rows(inbound, 0, COUNT, out_recv)
        gather(0)
        for begin, end in every:
            lanes = slice(begin * LANES, end * LANES)
            spectrum[:, lanes] = over_cells(0, lanes)

        scalars = line_green[pl.ds(line_me, 1), :]
        square_z = scalars[:, :LANES]
        gain_z = scalars[:, LANES:]
        for j in range(CHUNKS):
            squared = green[0, j] + square_z
            positive = squared > 0.0
            bounded = jnp.where(positive, squared, 1.0)
            multiplier[j] = jnp.where(positive, green[1, j] * gain_z / bounded, 0.0)

        wait_rows(inbound, 1, COUNT, out_recv)
        gather(1)
        for begin, end in every:
            lanes = slice(begin * LANES, end * LANES)
            block = spectrum[:, lanes] + over_cells(1, lanes)
            for j in range(begin, end):
                at = (j - begin) * LANES
                high, low = split(block[:, at : at + LANES] * multiplier[j])
                second_hi[:, j * LANES : (j + 1) * LANES] = high
                second_lo[:, j * LANES : (j + 1) * LANES] = low

        def send_row(group, other):
            pltpu.make_async_remote_copy(
                part(returning, group, other),
                part(returned, group, line_me),
                back_send.at[group],
                back_recv.at[group],
                device_id=(lax.div(other, N_PY), lax.rem(other, N_PY)),
                device_id_type=MESH,
            ).start()

        for group in range(2):
            for begin, end in pairs(group):
                lanes = slice(begin * LANES, end * LANES)
                block = product((second_hi[...], second_lo[...]), (cell_hi[:, lanes], cell_lo[:, lanes]), NN)
                block = jnp.concatenate(
                    [turned(block[:, (j - begin) * LANES : (j - begin + 1) * LANES], j) for j in range(begin, end)], axis=1
                )
                mixed = product(brick_pair, split(block), NN)
                for j in range(begin, end):
                    at = (j - begin) * LANES
                    upper = mixed[:COUNT, at : at + LANES]
                    crossed = swap(mixed[COUNT:, at : at + LANES])
                    returning[j] = jnp.where(left, upper, -upper) - crossed

            def send_back(step, carry, group=group):
                for k in range(5):
                    send_row(group, lax.rem(me + 1 + 5 * step + k, COUNT))
                return carry

            pltpu.make_async_copy(part(returning, group, me), part(returned, group, line_me), back_recv.at[group]).start()
            lax.fori_loop(0, (COUNT - 1) // 5, send_back, 0)

    def restore(group):
        begin, end = GROUPS[group][:2]
        wait_rows(returned, group, LINES, back_recv)
        for j in range(begin, end):
            high, low = split(returned[j].T)
            rows = slice(j * HALF, (j + 1) * HALF)
            turned_hi[rows, :PADDED] = high[:HALF]
            turned_hi[rows, PADDED:] = high[HALF:]
            turned_lo[rows, :PADDED] = low[:HALF]
            turned_lo[rows, PADDED:] = low[HALF:]
        rows = slice(begin * HALF, end * HALF)
        high, low = split(product((turned_hi[rows], turned_lo[rows]), (line_hi[...], line_lo[...]), NN))
        field_hi[rows] = high
        field_lo[rows] = low

    def sample(number, second):
        runs = runs_of(number, second)
        total = sum(end - begin for _, begin, end, _ in runs)
        if number < 2:
            first_at = runs[0][3]
            field = (field_hi[first_at : first_at + total], field_lo[first_at : first_at + total])
        else:
            field = tuple(
                jnp.concatenate([values[at : at + end - begin] for _, begin, end, at in runs], axis=0)
                for values in (field_hi, field_lo)
            )
        lanes = slice(2 * number * SLOTS, 2 * (number + 1) * SLOTS)
        sampled[:total] = product(field, (wz_hi[:, lanes], wz_lo[:, lanes]), NN)

        def block(step, carry):
            at = pl.multiple_of(step * LANES, LANES)
            here = pl.ds(at, LANES)
            found = {}
            row_at = 0
            for y, begin, end, _ in runs:
                rows = slice(row_at, row_at + end - begin)
                row_at += end - begin
                level = sampled[rows, here]
                rising = sampled[rows, pl.ds(SLOTS + at, LANES)]
                weight = wy[number, y : y + 1, here]
                terms = [weight * level, sy[number, y : y + 1, here] * level, weight * rising]
                before = found.get((begin, end))
                found[begin, end] = terms if before is None else [a + b for a, b in zip(before, terms)]
            sums = None
            for (begin, end), (over_y, slope_over_y, rising_over_y) in found.items():
                weight = wx[number, begin:end, here]
                terms = [weight * over_y, sx[number, begin:end, here] * over_y]
                terms += [weight * slope_over_y, weight * rising_over_y]
                terms = [jnp.sum(values, axis=0, keepdims=True) for values in terms]
                sums = terms if sums is None else [a + b for a, b in zip(sums, terms)]
            for row, total_row in enumerate(sums):
                if second:
                    total_row = total_row + partials[number, row : row + 1, here]
                partials[number, row : row + 1, here] = total_row
            return carry

        lax.fori_loop(0, SLOTS // LANES, block, 0)

    part_copies = []

    def give(number):
        step_x, step_y = CLASSES[number][:2]
        target = (lax.rem(px + N_PX - step_x, N_PX), lax.rem(py + N_PY - step_y, N_PY))
        copy = pltpu.make_async_remote_copy(
            partials.at[number],
            received.at[number],
            part_send.at[number],
            part_recv.at[number],
            device_id=target,
            device_id_type=MESH,
        )
        copy.start()
        part_copies.append(copy)

    restore(0)
    for number in range(1, 4):
        sample(number, False)
        give(number)
    sample(0, False)
    restore(1)
    sample(0, True)
    summed = partials[0, 0:4]
    for copy in part_copies:
        copy.wait_recv()
    for number in range(1, 4):
        summed = summed + received[number, 0:4]
    result[0, 0] = summed[0:1] * occupied
    for d in range(3):
        result[1 + d, 0] = -weighted * summed[1 + d : 2 + d]

    for copy in atom_copies + part_copies:
        copy.wait_send()

    @pl.when(active)
    def _():
        for group in range(2):
            wait_rows(outbound, group, LINES - 1, out_send)
            wait_rows(returning, group, COUNT - 1, back_send)

    @pl.when(jnp.logical_not(active))
    def _():
        for group in range(2):
            wait_rows(outbound, group, LINES, out_send)


def shards(charges, cells, fractions, filled):
    line = halves(line_table())
    brick = halves(brick_table())
    cell = halves(cell_table())
    twiddle = np.stack(twiddle_tables()).astype(np.float32)
    squares, gains, line_green = green_tables()
    green = np.stack([squares, gains]).astype(np.float32)
    constants = [*line, *brick, *cell, twiddle, green, line_green.astype(np.float32)]
    f32, bf16 = jnp.float32, jnp.bfloat16
    vmem = pltpu.VMEM
    message = vmem((CHUNKS, COUNT, LANES), f32)
    plane = vmem((COUNT, 2 * CELLS), bf16)
    whole = pl.BlockSpec(memory_space=pltpu.VMEM)
    distant = pl.BlockSpec(memory_space=pl.ANY)
    result = pl.pallas_call(
        kernel,
        out_shape=jax.ShapeDtypeStruct((4, 1, 1, SLOTS), f32),
        in_specs=[distant] * 3 + [whole] + [distant] * 9,
        out_specs=whole,
        scratch_shapes=[
            vmem((1, 1, SLOTS), f32),
            vmem((3, 1, 1, SLOTS), jnp.int32),
            vmem((3, 1, 1, SLOTS), f32),
            vmem((ROWS, 2 * LANES), f32),
            vmem((2 * PADDED, GRID), bf16),
            vmem((2 * PADDED, GRID), bf16),
            vmem((2 * COUNT, COUNT), bf16),
            vmem((2 * COUNT, COUNT), bf16),
            vmem((2 * CELLS, 2 * CELLS), bf16),
            vmem((2 * CELLS, 2 * CELLS), bf16),
            vmem((2, CHUNKS, COUNT, LANES), f32),
            vmem((2, CHUNKS, COUNT, LANES), f32),
            vmem((4, 8, SLOTS), f32),
            vmem((4, WIDE_X, SLOTS), f32),
            vmem((4, WIDE_X, SLOTS), f32),
            vmem((4, 16, SLOTS), f32),
            vmem((4, 16, SLOTS), f32),
            vmem((GRID, 8 * SLOTS), bf16),
            vmem((GRID, 8 * SLOTS), bf16),
            vmem((CELLS, SLOTS), bf16),
            vmem((CELLS, SLOTS), bf16),
            vmem((CELLS + HALF, GRID), f32),
            vmem((CHUNKS, ROWS, LANES), f32),
            message,
            message,
            plane,
            plane,
            plane,
            plane,
            message,
            message,
            vmem((CELLS, 2 * PADDED), bf16),
            vmem((CELLS, 2 * PADDED), bf16),
            vmem((CELLS, GRID), bf16),
            vmem((CELLS, GRID), bf16),
            vmem((COUNT, 2 * CELLS), f32),
            vmem((4, 2, ORDER, 16, SLOTS), bf16),
            vmem((4, 2, ORDER, 16, SLOTS), bf16),
            vmem((4, 16, SLOTS), jnp.int16),
            vmem((CELLS, 2 * SLOTS), f32),
            vmem((4, 8, SLOTS), f32),
            vmem((4, 8, SLOTS), f32),
            pltpu.SemaphoreType.DMA((12,)),
            pltpu.SemaphoreType.DMA((4,)),
            pltpu.SemaphoreType.DMA((4,)),
            pltpu.SemaphoreType.DMA((2,)),
            pltpu.SemaphoreType.DMA((2,)),
            pltpu.SemaphoreType.DMA((2,)),
            pltpu.SemaphoreType.DMA((2,)),
            pltpu.SemaphoreType.DMA((4,)),
            pltpu.SemaphoreType.DMA((4,)),
            pltpu.SemaphoreType.REGULAR,
        ],
        compiler_params=pltpu.CompilerParams(
            collective_id=0, has_side_effects=True, vmem_limit_bytes=56 * 1024 * 1024
        ),
    )(charges, cells, fractions, filled, *[jnp.asarray(table) for table in constants])
    return pl.pallas_call(
        hand_over,
        out_shape=(jax.ShapeDtypeStruct((1, 1, SLOTS), f32), jax.ShapeDtypeStruct((3, 1, 1, SLOTS), f32)),
        in_specs=[whole],
        out_specs=(whole, whole),
    )(result)


def solution(mesh):
    placed = (
        P("px", "py", None),
        P(None, "px", "py", None),
        P(None, "px", "py", None),
        P("px", "py"),
    )
    return jax.shard_map(
        shards,
        mesh=mesh,
        in_specs=placed,
        out_specs=(P("px", "py", None), P(None, "px", "py", None)),
        check_vma=False,
    )
```

```python
import math

import jax
import jax.numpy as jnp
import ml_dtypes
import numpy as np
from jax import lax
from jax.experimental import pallas as pl
from jax.experimental.pallas import tpu as pltpu
from jax.sharding import PartitionSpec as P

GRID = 384
ORDER = 6
SLOTS = 512
N_PX = 8
N_PY = 32
COUNT = N_PX * N_PY
WIDE_X = GRID // N_PX
WIDE_Y = GRID // N_PY
CELLS = WIDE_X * WIDE_Y
LINES = GRID // 2 + 1
HALF = 64
LANES = 128
CHUNKS = CELLS // HALF
ROWS = 208
PADDED = 256
EDGE_X = 16
EDGE_Y = 5
SPLITTING = 1.6
COUPLING = 1.0 / math.pi
MESH = pl.DeviceIdType.MESH
NT = (((1,), (1,)), ((), ()))
NN = (((1,), (0,)), ((), ()))
GROUPS = ((0, 6), (6, 9))
FULL_Y = 6
RUNS = (
    [((y, 0, WIDE_X), y * WIDE_X) for y in range(FULL_Y)]
    + [((y, 0, EDGE_X), FULL_Y * WIDE_X + (y - FULL_Y) * EDGE_X) for y in range(FULL_Y, WIDE_Y)]
    + [((y, EDGE_X, WIDE_X), 2 * CELLS // 3 + (y - FULL_Y) * (WIDE_X - EDGE_X)) for y in range(FULL_Y, WIDE_Y)]
)
CELL_Y = np.concatenate([np.full(end - begin, y) for (y, begin, end), _ in RUNS])
CELL_X = np.concatenate([np.arange(begin, end) for (_, begin, end), _ in RUNS])
CLASSES = ((0, 0, WIDE_X, WIDE_Y), (0, 1, WIDE_X, EDGE_Y), (1, 0, EDGE_X, WIDE_Y), (1, 1, EDGE_X, EDGE_Y))


def halves(table):
    high = table.astype(ml_dtypes.bfloat16)
    low = (table - high.astype(np.float64)).astype(ml_dtypes.bfloat16)
    return high, low


def chunked(first, second):
    rows = first.shape[0]
    pair = np.stack([first.reshape(rows, CHUNKS, HALF), second.reshape(rows, CHUNKS, HALF)], axis=2)
    return np.ascontiguousarray(pair.reshape(rows, CHUNKS, LANES).transpose(1, 0, 2))


def turn(numerators, period):
    return 2.0 * math.pi / period * np.mod(numerators, period).astype(np.float64)


def line_table():
    at = np.arange(GRID)
    angles = turn(np.arange(LINES)[:, None] * at[None, :], GRID)
    table = np.zeros((2, PADDED, GRID))
    table[0, :LINES] = np.cos(angles)
    table[1, :LINES] = -np.sin(angles)
    return table.reshape(2 * PADDED, GRID)


def brick_table():
    device = np.arange(COUNT)
    a, b = device // N_PY, device % N_PY
    angles = turn(4 * a[:, None] * a[None, :] + b[:, None] * b[None, :], N_PY)
    return np.concatenate([np.cos(angles), -np.sin(angles)])


def twiddle_tables():
    device = np.arange(COUNT)
    a, b = device // N_PY, device % N_PY
    y, x = CELL_Y, CELL_X
    angles = turn(a[:, None] * x[None, :] + b[:, None] * y[None, :], GRID)
    cosines, sines = np.cos(angles), -np.sin(angles)
    return chunked(cosines, cosines), chunked(-sines, sines)


def cell_table():
    y, x = CELL_Y, CELL_X
    angles = turn(4 * y[:, None] * y[None, :] + x[:, None] * x[None, :], WIDE_X)
    cosines, sines = np.cos(angles), -np.sin(angles)
    table = np.zeros((CHUNKS, 2, HALF, CHUNKS, 2, HALF))
    shape = (CHUNKS, HALF, CHUNKS, HALF)
    table[:, 0, :, :, 0, :] = cosines.reshape(shape)
    table[:, 0, :, :, 1, :] = sines.reshape(shape)
    table[:, 1, :, :, 0, :] = -sines.reshape(shape)
    table[:, 1, :, :, 1, :] = cosines.reshape(shape)
    return table.reshape(2 * CELLS, 2 * CELLS)


def axis_terms(indices):
    signed = np.where(indices <= GRID // 2, indices, indices - GRID) / GRID
    values = [1.0, 0.0]
    for k in range(2, ORDER):
        values = [
            ((k - j) * (values[j - 1] if j >= 1 else 0.0) + (1.0 + j) * (values[j] if j < k else 0.0)) / k
            for j in range(k + 1)
        ]
    total = sum(values[j] * np.exp(1j * turn(indices * j, GRID)) for j in range(ORDER - 1))
    return signed * signed, 1.0 / np.abs(total) ** 2


def green_tables():
    device = np.arange(COUNT)
    freq_x = (device // N_PY)[:, None] + N_PX * CELL_X[None, :]
    freq_y = (device % N_PY)[:, None] + N_PY * CELL_Y[None, :]
    square_x, modulus_x = axis_terms(freq_x)
    square_y, modulus_y = axis_terms(freq_y)
    squares = square_x + square_y
    rate = math.pi * math.pi / (SPLITTING * SPLITTING)
    gains = np.exp(-rate * squares) * modulus_x * modulus_y
    square_z, modulus_z = axis_terms(np.arange(LINES))
    weight = np.full(LINES, 2.0)
    weight[0] = weight[-1] = 1.0
    factor = COUPLING / float(GRID) ** 3
    line = np.zeros((ROWS, 2, LANES))
    line[:LINES, 0] = square_z[:, None]
    line[:LINES, 1] = (factor * weight * np.exp(-rate * square_z) * modulus_z)[:, None]
    return chunked(squares, squares), chunked(gains, -gains), line.reshape(ROWS, 2 * LANES)


def split(value):
    high = value.astype(jnp.bfloat16)
    return high, (value - high.astype(jnp.float32)).astype(jnp.bfloat16)


def product(left, right, dims):
    def one(a, b):
        return lax.dot_general(a, b, dims, preferred_element_type=jnp.float32)

    rows = left[0].shape[0]
    both = one(jnp.concatenate([left[0], left[1]], axis=0), right[0])
    return both[:rows] + both[rows:] + one(left[0], right[1])


def spline_rows(fraction):
    values = [1.0 - fraction, fraction]
    previous = values
    for k in range(2, ORDER):
        previous = values
        updated = []
        for j in range(k + 1):
            terms = []
            if j >= 1:
                terms.append((fraction + float(k - j)) * previous[j - 1])
            if j < k:
                terms.append((float(1 + j) - fraction) * previous[j])
            updated.append(sum(terms[1:], terms[0]) * (1.0 / k))
        values = updated
    slopes = []
    for j in range(ORDER):
        if j == 0:
            slopes.append(-previous[0])
        elif j == ORDER - 1:
            slopes.append(previous[j - 1])
        else:
            slopes.append(previous[j - 1] - previous[j])
    return values, slopes


def place(offset, rows):
    total = jnp.zeros(offset.shape, jnp.float32)
    for j in range(ORDER):
        total = jnp.where(offset == j, rows[j], total)
    return total


def runs_of(number, second):
    size_x, size_y = CLASSES[number][2:]
    found = []
    for (y, begin, end), at in RUNS:
        if (at >= 2 * CELLS // 3) == second and y < size_y and begin < size_x:
            found.append((y, begin, min(end, size_x), at))
    return found


def swap(value):
    return pltpu.roll(value, HALF, 1)


def hand_over(result, potentials, forces):
    potentials[...] = result[0]
    forces[...] = result[1:4]


def kernel(
    charges_any,
    cells_any,
    fractions_any,
    filled,
    line_hi_any,
    line_lo_any,
    brick_hi_any,
    brick_lo_any,
    cell_hi_any,
    cell_lo_any,
    twiddle_any,
    green_any,
    line_green_any,
    result,
    charges,
    cells,
    fractions,
    line_green,
    line_hi,
    line_lo,
    brick_hi,
    brick_lo,
    cell_hi,
    cell_lo,
    twiddle,
    green,
    atoms,
    wx,
    sx,
    wy,
    sy,
    wz_hi,
    wz_lo,
    column_hi,
    column_lo,
    grid,
    outbound,
    inbound,
    multiplier,
    first_hi,
    first_lo,
    second_hi,
    second_lo,
    returning,
    returned,
    turned_hi,
    turned_lo,
    field_hi,
    field_lo,
    spectrum,
    taps_hi,
    taps_lo,
    offsets,
    sampled,
    partials,
    received,
    table_sems,
    atom_send,
    atom_recv,
    out_send,
    out_recv,
    back_send,
    back_recv,
    part_send,
    part_recv,
    vouched,
):
    px = lax.axis_index("px")
    py = lax.axis_index("py")
    me = px * N_PY + py

    arguments = [
        pltpu.make_async_copy(source, target, table_sems.at[9 + number])
        for number, (source, target) in enumerate(
            [(charges_any, charges), (cells_any, cells), (fractions_any, fractions)]
        )
    ]
    for copy in arguments:
        copy.start()

    barrier = pltpu.get_barrier_semaphore()

    def greet(target):
        pl.semaphore_signal(barrier, inc=1, device_id=target, device_id_type=MESH)

    def greet_row(step, carry):
        greet((px, lax.rem(py + step, N_PY)))
        return carry

    def greet_column(step, carry):
        greet((lax.rem(px + step, N_PX), py))
        return carry

    greet((lax.rem(px + 1, N_PX), lax.rem(py + 1, N_PY)))
    greet((lax.rem(px + N_PX - 1, N_PX), lax.rem(py + N_PY - 1, N_PY)))
    lax.fori_loop(1, N_PX, greet_column, 0)
    lax.fori_loop(1, N_PY, greet_row, 0)

    tables = [
        pltpu.make_async_copy(source, target, table_sems.at[number])
        for number, (source, target) in enumerate(
            [
                (line_hi_any, line_hi),
                (line_lo_any, line_lo),
                (brick_hi_any, brick_hi),
                (brick_lo_any, brick_lo),
                (twiddle_any, twiddle),
                (green_any, green),
                (cell_hi_any, cell_hi),
                (cell_lo_any, cell_lo),
                (line_green_any, line_green),
            ]
        )
    ]
    for table in tables:
        table.start()
    for copy in arguments:
        copy.wait()

    slot = lax.broadcasted_iota(jnp.int32, (1, SLOTS), 1)
    occupied = (slot < filled[...]).astype(jnp.float32)
    weighted = charges[0] * occupied
    atoms[0, 0:1] = weighted
    for d in range(3):
        atoms[0, 1 + d : 2 + d] = cells[d, 0].astype(jnp.float32)
        atoms[0, 4 + d : 5 + d] = fractions[d, 0]
    atoms[0, 7:8] = jnp.zeros((1, SLOTS), jnp.float32)
    returned[:, LINES - 1 :, :] = jnp.zeros((CHUNKS, PADDED - LINES + 1, LANES), jnp.float32)

    def side_tables(number):
        step_x, step_y, size_x, size_y = CLASSES[number]
        values, slopes = spline_rows(atoms[number, 4:7])
        depth_rows(number, values, slopes)
        for row, step, wide, size, weights, rises in (
            (0, step_x, WIDE_X, size_x, wx, sx),
            (1, step_y, WIDE_Y, 16, wy, sy),
        ):
            start = atoms[number, 1 + row : 2 + row].astype(jnp.int32) - step * wide
            offset = lax.broadcasted_iota(jnp.int32, (size, SLOTS), 0) - start
            weights[number, :size] = place(offset, [v[row : row + 1] for v in values])
            rises[number, :size] = place(offset, [v[row : row + 1] for v in slopes])

    def depth_rows(number, values, slopes):
        for kind, rows in enumerate((values, slopes)):
            for j in range(ORDER):
                high, low = split(jnp.broadcast_to(rows[j][2:3], (16, SLOTS)))
                taps_hi[number, kind, j] = high
                taps_lo[number, kind, j] = low
        start = atoms[number, 3:4].astype(jnp.int32)
        offsets[number] = (lax.broadcasted_iota(jnp.int32, (16, SLOTS), 0) - start).astype(jnp.int16)

    def depth_block(number, kind, at, lanes):
        offset = offsets[number] + jnp.full((16, SLOTS), at, jnp.int32).astype(jnp.int16)
        offset = jnp.where(offset < 0, offset + jnp.int16(GRID), offset)
        high = jnp.zeros((16, SLOTS), jnp.bfloat16)
        low = high
        for j in range(ORDER):
            here = offset == j
            high = jnp.where(here, taps_hi[number, kind, j], high)
            low = jnp.where(here, taps_lo[number, kind, j], low)
        wz_hi[pl.ds(at, 16), lanes] = high
        wz_lo[pl.ds(at, 16), lanes] = low

    def depth_tables(number):
        def block(step, carry):
            depth_block(number, 0, pl.multiple_of(step * 16, 16), pl.ds(2 * number * SLOTS, SLOTS))
            return carry

        lax.fori_loop(0, GRID // 16, block, 0)

    def slope_block(step):
        step = jnp.minimum(step, 4 * GRID // 32 - 1)
        number = lax.div(step, GRID // 32)
        at = lax.rem(step, GRID // 32) * 32
        lanes = pl.ds(pl.multiple_of((2 * number + 1) * SLOTS, SLOTS), SLOTS)
        for k in range(2):
            depth_block(number, 1, pl.multiple_of(at + 16 * k, 16), lanes)

    def spread(number, second):
        charge = atoms[number, 0:1]
        total = 0
        for y, begin, end, _ in runs_of(number, second):
            high, low = split((wx[number, begin:end] * charge) * wy[number, y : y + 1])
            column_hi[total : total + end - begin] = high
            column_lo[total : total + end - begin] = low
            total += end - begin
        lanes = pl.ds(2 * number * SLOTS, SLOTS)
        return product((column_hi[:total], column_lo[:total]), (wz_hi[:, lanes], wz_lo[:, lanes]), NT)

    pl.semaphore_wait(barrier, N_PX + N_PY)

    atom_copies = []
    for number in range(1, 4):
        step_x, step_y = CLASSES[number][:2]
        target = (lax.rem(px + step_x, N_PX), lax.rem(py + step_y, N_PY))
        copy = pltpu.make_async_remote_copy(
            atoms.at[0], atoms.at[number], atom_send.at[number], atom_recv.at[number], device_id=target, device_id_type=MESH
        )
        copy.start()
        atom_copies.append(copy)

    def vouch(step, carry):
        pl.semaphore_signal(vouched, inc=1, device_id=(lax.rem(px + step, N_PX), py), device_id_type=MESH)
        return carry

    lax.fori_loop(1, N_PX, vouch, 0)

    side_tables(0)
    depth_tables(0)

    def spread_near(number):
        added = spread(number, False)
        place_at = 0
        for _, begin, end, at in runs_of(number, False):
            grid[at : at + end - begin] += added[place_at : place_at + end - begin]
            place_at += end - begin

    def transform(begin, end):
        lanes = end - begin + (end - begin) % 2
        dense = split(grid[begin * HALF : (begin + lanes) * HALF])
        cosine_part = product((line_hi[:ROWS], line_lo[:ROWS]), dense, NT)
        sine_part = product((line_hi[PADDED : PADDED + ROWS], line_lo[PADDED : PADDED + ROWS]), dense, NT)
        lower = lax.broadcasted_iota(jnp.int32, (ROWS, LANES), 1) < HALF
        for j in range(begin, end):
            at = ((j - begin) // 2) * LANES
            cosine_block = cosine_part[:, at : at + LANES]
            sine_block = sine_part[:, at : at + LANES]
            if (j - begin) % 2 == 0:
                outbound[j] = jnp.where(lower, cosine_block, swap(sine_block))
            else:
                outbound[j] = jnp.where(lower, swap(cosine_block), sine_block)

    first, second = GROUPS
    grid[: first[1] * HALF] = spread(0, False)
    grid[CELLS:] = jnp.zeros((HALF, GRID), jnp.float32)
    for number in range(1, 4):
        atom_copies[number - 1].wait_recv()
        side_tables(number)
        depth_tables(number)
        spread_near(number)
    tables[0].wait()
    tables[1].wait()
    transform(*first)
    pl.semaphore_wait(vouched, N_PX - 1)

    core_me = lax.rem(px, 2)
    low_me = lax.div(px, 2)
    z_me = 4 * lax.div(py, 16) + low_me
    x_me = lax.rem(lax.div(py, 4), 4)
    y_me = lax.rem(py, 4)

    def main_core(low, to_y):
        return lax.rem(low + lax.div(to_y, 8) + lax.div(lax.rem(to_y, 4), 2), 2)

    order = low_me * N_PY + py
    main_me = main_core(low_me, py)
    other_me = lax.rem(core_me + main_me, 2)
    last = jnp.logical_and(px == 1, py == 1)
    matching = jnp.logical_and(other_me == 1, lax.rem(low_me + x_me + y_me, 2) == 0)
    active = jnp.logical_or(jnp.logical_or(other_me == 0, last), matching)
    line_me = (1 - other_me) * order + other_me * (128 + lax.div(order, 2))
    line_me = line_me + last.astype(jnp.int32) * (LINES - 1 - 128)

    def part(buffer, group, row):
        begin, end = GROUPS[group][:2]
        return buffer.at[pl.ds(begin, end - begin), pl.ds(row, 1), :]

    def keep_line(group):
        pltpu.make_async_copy(part(outbound, group, line_me), part(inbound, group, me), out_recv.at[group]).start()

    def send_line(group, line, to_x, to_y):
        pltpu.make_async_remote_copy(
            part(outbound, group, line),
            part(inbound, group, me),
            out_send.at[group],
            out_recv.at[group],
            device_id=(to_x, to_y),
            device_id_type=MESH,
        ).start()

    def move_along_z(phase):
        far = lax.div(phase + 1, 2)
        return 4 + (2 * lax.rem(phase, 2) - 1) * -far

    def send_even(group, low, high, x, move_y):
        to_y = 16 * high + 4 * x + lax.rem(y_me + move_y, 4)
        send_line(group, N_PY * low + to_y, 2 * low + main_core(low, to_y), to_y)

    def send_odd(group, low, high, x, move_pair):
        pair = lax.rem(lax.div(y_me, 2) + move_pair, 2)
        to_y = 16 * high + 4 * x + 2 * pair + lax.rem(low + x, 2)
        line = 128 + 16 * low + 8 * high + 2 * x + pair
        send_line(group, line, 2 * low + 1 - main_core(low, to_y), to_y)

    def send_group(group):
        def send_column(move_z, move_x, skip=0):
            z = lax.rem(z_me + move_z, 8)
            low, high = lax.rem(z, 4), lax.div(z, 4)
            x = lax.rem(x_me + move_x, 4)
            for k in range(skip, 4):
                send_even(group, low, high, x, k)
            for k in range(min(skip, 1), 2):
                send_odd(group, low, high, x, k)

        def send_far(step, carry):
            send_column(move_along_z(lax.div(step, 4)), lax.rem(step, 4))
            slope_block(28 * group + step)
            return carry

        def send_near(step, carry):
            send_column(0, step)
            return carry

        lax.fori_loop(0, 28, send_far, 0)
        lax.fori_loop(1, 4, send_near, 0)
        send_column(0, 0, skip=1)
        high = lax.div(py, 16)
        pl.when(active)(lambda: keep_line(group))
        pl.when(other_me == 1)(lambda: send_even(group, low_me, high, x_me, 0))
        pl.when(jnp.logical_not(matching))(lambda: send_odd(group, low_me, high, x_me, 0))
        pl.when(jnp.logical_not(last))(lambda: send_line(group, LINES - 1, 1, 1))

    send_group(0)
    grid[second[0] * HALF : CELLS] = spread(0, True)
    transform(*second)
    send_group(1)

    for table in tables[2:]:
        table.wait()

    def wait_rows(buffer, group, count, semaphores):
        begin, end = GROUPS[group][:2]
        view = buffer.at[pl.ds(begin, end - begin), pl.ds(0, count), :]
        pltpu.make_async_copy(view, view, semaphores.at[group]).wait()

    @pl.when(active)
    def _():
        left = lax.broadcasted_iota(jnp.int32, (COUNT, LANES), 1) < HALF
        brick_pair = (brick_hi[...], brick_lo[...])

        def pairs(group):
            begin, end = GROUPS[group][:2]
            return [(j, min(j + 2, end)) for j in range(begin, end, 2)]

        def turned(value, j):
            return value * twiddle[0, j] + swap(value) * twiddle[1, j]

        def gather(group):
            for begin, end in pairs(group):
                block = jnp.concatenate([inbound[j] for j in range(begin, end)], axis=1)
                mixed = product(brick_pair, split(block), NN)
                for j in range(begin, end):
                    at = (j - begin) * LANES
                    upper = mixed[:COUNT, at : at + LANES]
                    crossed = swap(mixed[COUNT:, at : at + LANES])
                    value = upper + jnp.where(left, -crossed, crossed)
                    high, low = split(turned(value, j))
                    first_hi[:, j * LANES : (j + 1) * LANES] = high
                    first_lo[:, j * LANES : (j + 1) * LANES] = low

        def over_cells(group, lanes):
            rows = slice(GROUPS[group][0] * LANES, GROUPS[group][1] * LANES)
            return product((first_hi[:, rows], first_lo[:, rows]), (cell_hi[rows, lanes], cell_lo[rows, lanes]), NN)

        every = pairs(0) + pairs(1)
        wait_rows(inbound, 0, COUNT, out_recv)
        gather(0)
        for begin, end in every:
            lanes = slice(begin * LANES, end * LANES)
            spectrum[:, lanes] = over_cells(0, lanes)

        scalars = line_green[pl.ds(line_me, 1), :]
        square_z = scalars[:, :LANES]
        gain_z = scalars[:, LANES:]
        for j in range(CHUNKS):
            squared = green[0, j] + square_z
            positive = squared > 0.0
            bounded = jnp.where(positive, squared, 1.0)
            multiplier[j] = jnp.where(positive, green[1, j] * gain_z / bounded, 0.0)

        wait_rows(inbound, 1, COUNT, out_recv)
        gather(1)
        for begin, end in every:
            lanes = slice(begin * LANES, end * LANES)
            block = spectrum[:, lanes] + over_cells(1, lanes)
            for j in range(begin, end):
                at = (j - begin) * LANES
                high, low = split(block[:, at : at + LANES] * multiplier[j])
                second_hi[:, j * LANES : (j + 1) * LANES] = high
                second_lo[:, j * LANES : (j + 1) * LANES] = low

        def send_row(group, to_x, to_y):
            other = N_PY * to_x + to_y
            pltpu.make_async_remote_copy(
                part(returning, group, other),
                part(returned, group, line_me),
                back_send.at[group],
                back_recv.at[group],
                device_id=(to_x, to_y),
                device_id_type=MESH,
            ).start()

        def send_rows(group, move_core, move_z, move_x, skip=0):
            z = lax.rem(z_me + move_z, 8)
            to_x = 2 * lax.rem(z, 4) + lax.rem(core_me + move_core, 2)
            base = 16 * lax.div(z, 4) + 4 * lax.rem(x_me + move_x, 4)
            for k in range(skip, 4):
                send_row(group, to_x, base + lax.rem(y_me + k, 4))

        for group in range(2):
            for begin, end in pairs(group):
                lanes = slice(begin * LANES, end * LANES)
                block = product((second_hi[...], second_lo[...]), (cell_hi[:, lanes], cell_lo[:, lanes]), NN)
                block = jnp.concatenate(
                    [turned(block[:, (j - begin) * LANES : (j - begin + 1) * LANES], j) for j in range(begin, end)], axis=1
                )
                mixed = product(brick_pair, split(block), NN)
                for j in range(begin, end):
                    at = (j - begin) * LANES
                    upper = mixed[:COUNT, at : at + LANES]
                    crossed = swap(mixed[COUNT:, at : at + LANES])
                    returning[j] = jnp.where(left, upper, -upper) - crossed

            def send_far(step, carry, group=group):
                phase = lax.div(step, 8)
                send_rows(group, lax.rem(lax.div(step, 4), 2), move_along_z(phase), lax.rem(step, 4))
                return carry

            def send_near(step, carry, group=group):
                send_rows(group, lax.div(step, 4), 0, lax.rem(step, 4))
                return carry

            lax.fori_loop(0, 56, send_far, 0)
            lax.fori_loop(1, 8, send_near, 0)
            send_rows(group, 0, 0, 0, skip=1)
            pltpu.make_async_copy(part(returning, group, me), part(returned, group, line_me), back_recv.at[group]).start()

    def restore(group):
        begin, end = GROUPS[group][:2]
        wait_rows(returned, group, LINES, back_recv)
        for j in range(begin, end):
            high, low = split(returned[j].T)
            rows = slice(j * HALF, (j + 1) * HALF)
            turned_hi[rows, :PADDED] = high[:HALF]
            turned_hi[rows, PADDED:] = high[HALF:]
            turned_lo[rows, :PADDED] = low[:HALF]
            turned_lo[rows, PADDED:] = low[HALF:]
        rows = slice(begin * HALF, end * HALF)
        high, low = split(product((turned_hi[rows], turned_lo[rows]), (line_hi[...], line_lo[...]), NN))
        field_hi[rows] = high
        field_lo[rows] = low

    def sample(number, second):
        runs = runs_of(number, second)
        total = sum(end - begin for _, begin, end, _ in runs)
        if number < 2:
            first_at = runs[0][3]
            field = (field_hi[first_at : first_at + total], field_lo[first_at : first_at + total])
        else:
            field = tuple(
                jnp.concatenate([values[at : at + end - begin] for _, begin, end, at in runs], axis=0)
                for values in (field_hi, field_lo)
            )
        lanes = slice(2 * number * SLOTS, 2 * (number + 1) * SLOTS)
        sampled[:total] = product(field, (wz_hi[:, lanes], wz_lo[:, lanes]), NN)

        def block(step, carry):
            at = pl.multiple_of(step * LANES, LANES)
            here = pl.ds(at, LANES)
            found = {}
            row_at = 0
            for y, begin, end, _ in runs:
                rows = slice(row_at, row_at + end - begin)
                row_at += end - begin
                level = sampled[rows, here]
                rising = sampled[rows, pl.ds(SLOTS + at, LANES)]
                weight = wy[number, y : y + 1, here]
                terms = [weight * level, sy[number, y : y + 1, here] * level, weight * rising]
                before = found.get((begin, end))
                found[begin, end] = terms if before is None else [a + b for a, b in zip(before, terms)]
            sums = None
            for (begin, end), (over_y, slope_over_y, rising_over_y) in found.items():
                weight = wx[number, begin:end, here]
                terms = [weight * over_y, sx[number, begin:end, here] * over_y]
                terms += [weight * slope_over_y, weight * rising_over_y]
                terms = [jnp.sum(values, axis=0, keepdims=True) for values in terms]
                sums = terms if sums is None else [a + b for a, b in zip(sums, terms)]
            for row, total_row in enumerate(sums):
                if second:
                    total_row = total_row + partials[number, row : row + 1, here]
                partials[number, row : row + 1, here] = total_row
            return carry

        lax.fori_loop(0, SLOTS // LANES, block, 0)

    part_copies = []

    def give(number):
        step_x, step_y = CLASSES[number][:2]
        target = (lax.rem(px + N_PX - step_x, N_PX), lax.rem(py + N_PY - step_y, N_PY))
        copy = pltpu.make_async_remote_copy(
            partials.at[number],
            received.at[number],
            part_send.at[number],
            part_recv.at[number],
            device_id=target,
            device_id_type=MESH,
        )
        copy.start()
        part_copies.append(copy)

    restore(0)
    for number in range(1, 4):
        sample(number, False)
        give(number)
    sample(0, False)
    restore(1)
    sample(0, True)
    summed = partials[0, 0:4]
    for copy in part_copies:
        copy.wait_recv()
    for number in range(1, 4):
        summed = summed + received[number, 0:4]
    result[0, 0] = summed[0:1] * occupied
    for d in range(3):
        result[1 + d, 0] = -weighted * summed[1 + d : 2 + d]

    for copy in atom_copies + part_copies:
        copy.wait_send()

    @pl.when(active)
    def _():
        for group in range(2):
            wait_rows(outbound, group, LINES - 1, out_send)
            wait_rows(returning, group, COUNT - 1, back_send)

    @pl.when(jnp.logical_not(active))
    def _():
        for group in range(2):
            wait_rows(outbound, group, LINES, out_send)


def shards(charges, cells, fractions, filled):
    line = halves(line_table())
    brick = halves(brick_table())
    cell = halves(cell_table())
    twiddle = np.stack(twiddle_tables()).astype(np.float32)
    squares, gains, line_green = green_tables()
    green = np.stack([squares, gains]).astype(np.float32)
    constants = [*line, *brick, *cell, twiddle, green, line_green.astype(np.float32)]
    f32, bf16 = jnp.float32, jnp.bfloat16
    vmem = pltpu.VMEM
    message = vmem((CHUNKS, COUNT, LANES), f32)
    plane = vmem((COUNT, 2 * CELLS), bf16)
    whole = pl.BlockSpec(memory_space=pltpu.VMEM)
    distant = pl.BlockSpec(memory_space=pl.ANY)
    result = pl.pallas_call(
        kernel,
        out_shape=jax.ShapeDtypeStruct((4, 1, 1, SLOTS), f32),
        in_specs=[distant] * 3 + [whole] + [distant] * 9,
        out_specs=whole,
        scratch_shapes=[
            vmem((1, 1, SLOTS), f32),
            vmem((3, 1, 1, SLOTS), jnp.int32),
            vmem((3, 1, 1, SLOTS), f32),
            vmem((ROWS, 2 * LANES), f32),
            vmem((2 * PADDED, GRID), bf16),
            vmem((2 * PADDED, GRID), bf16),
            vmem((2 * COUNT, COUNT), bf16),
            vmem((2 * COUNT, COUNT), bf16),
            vmem((2 * CELLS, 2 * CELLS), bf16),
            vmem((2 * CELLS, 2 * CELLS), bf16),
            vmem((2, CHUNKS, COUNT, LANES), f32),
            vmem((2, CHUNKS, COUNT, LANES), f32),
            vmem((4, 8, SLOTS), f32),
            vmem((4, WIDE_X, SLOTS), f32),
            vmem((4, WIDE_X, SLOTS), f32),
            vmem((4, 16, SLOTS), f32),
            vmem((4, 16, SLOTS), f32),
            vmem((GRID, 8 * SLOTS), bf16),
            vmem((GRID, 8 * SLOTS), bf16),
            vmem((CELLS, SLOTS), bf16),
            vmem((CELLS, SLOTS), bf16),
            vmem((CELLS + HALF, GRID), f32),
            vmem((CHUNKS, ROWS, LANES), f32),
            message,
            message,
            plane,
            plane,
            plane,
            plane,
            message,
            message,
            vmem((CELLS, 2 * PADDED), bf16),
            vmem((CELLS, 2 * PADDED), bf16),
            vmem((CELLS, GRID), bf16),
            vmem((CELLS, GRID), bf16),
            vmem((COUNT, 2 * CELLS), f32),
            vmem((4, 2, ORDER, 16, SLOTS), bf16),
            vmem((4, 2, ORDER, 16, SLOTS), bf16),
            vmem((4, 16, SLOTS), jnp.int16),
            vmem((CELLS, 2 * SLOTS), f32),
            vmem((4, 8, SLOTS), f32),
            vmem((4, 8, SLOTS), f32),
            pltpu.SemaphoreType.DMA((12,)),
            pltpu.SemaphoreType.DMA((4,)),
            pltpu.SemaphoreType.DMA((4,)),
            pltpu.SemaphoreType.DMA((2,)),
            pltpu.SemaphoreType.DMA((2,)),
            pltpu.SemaphoreType.DMA((2,)),
            pltpu.SemaphoreType.DMA((2,)),
            pltpu.SemaphoreType.DMA((4,)),
            pltpu.SemaphoreType.DMA((4,)),
            pltpu.SemaphoreType.REGULAR,
        ],
        compiler_params=pltpu.CompilerParams(
            collective_id=0, has_side_effects=True, vmem_limit_bytes=56 * 1024 * 1024
        ),
    )(charges, cells, fractions, filled, *[jnp.asarray(table) for table in constants])
    return pl.pallas_call(
        hand_over,
        out_shape=(jax.ShapeDtypeStruct((1, 1, SLOTS), f32), jax.ShapeDtypeStruct((3, 1, 1, SLOTS), f32)),
        in_specs=[whole],
        out_specs=(whole, whole),
    )(result)


def solution(mesh):
    placed = (
        P("px", "py", None),
        P(None, "px", "py", None),
        P(None, "px", "py", None),
        P("px", "py"),
    )
    return jax.shard_map(
        shards,
        mesh=mesh,
        in_specs=placed,
        out_specs=(P("px", "py", None), P(None, "px", "py", None)),
        check_vma=False,
    )
```

```python
import math

import jax
import jax.numpy as jnp
import ml_dtypes
import numpy as np
from jax import lax
from jax.experimental import pallas as pl
from jax.experimental.pallas import tpu as pltpu
from jax.sharding import PartitionSpec as P

GRID = 384
ORDER = 6
SLOTS = 512
N_PX = 8
N_PY = 32
COUNT = N_PX * N_PY
WIDE_X = GRID // N_PX
WIDE_Y = GRID // N_PY
CELLS = WIDE_X * WIDE_Y
LINES = GRID // 2 + 1
HALF = 64
LANES = 128
CHUNKS = CELLS // HALF
ROWS = 208
PADDED = 256
EDGE_X = 16
EDGE_Y = 5
SPLITTING = 1.6
COUPLING = 1.0 / math.pi
MESH = pl.DeviceIdType.MESH
NT = (((1,), (1,)), ((), ()))
NN = (((1,), (0,)), ((), ()))
GROUPS = ((0, 6), (6, 9))
FULL_Y = 6
RUNS = (
    [((y, 0, WIDE_X), y * WIDE_X) for y in range(FULL_Y)]
    + [((y, 0, EDGE_X), FULL_Y * WIDE_X + (y - FULL_Y) * EDGE_X) for y in range(FULL_Y, WIDE_Y)]
    + [((y, EDGE_X, WIDE_X), 2 * CELLS // 3 + (y - FULL_Y) * (WIDE_X - EDGE_X)) for y in range(FULL_Y, WIDE_Y)]
)
CELL_Y = np.concatenate([np.full(end - begin, y) for (y, begin, end), _ in RUNS])
CELL_X = np.concatenate([np.arange(begin, end) for (_, begin, end), _ in RUNS])
CLASSES = ((0, 0, WIDE_X, WIDE_Y), (0, 1, WIDE_X, EDGE_Y), (1, 0, EDGE_X, WIDE_Y), (1, 1, EDGE_X, EDGE_Y))


def halves(table):
    high = table.astype(ml_dtypes.bfloat16)
    low = (table - high.astype(np.float64)).astype(ml_dtypes.bfloat16)
    return high, low


def chunked(first, second):
    rows = first.shape[0]
    pair = np.stack([first.reshape(rows, CHUNKS, HALF), second.reshape(rows, CHUNKS, HALF)], axis=2)
    return np.ascontiguousarray(pair.reshape(rows, CHUNKS, LANES).transpose(1, 0, 2))


def turn(numerators, period):
    return 2.0 * math.pi / period * np.mod(numerators, period).astype(np.float64)


def line_table():
    at = np.arange(GRID)
    angles = turn(np.arange(LINES)[:, None] * at[None, :], GRID)
    table = np.zeros((2, PADDED, GRID))
    table[0, :LINES] = np.cos(angles)
    table[1, :LINES] = -np.sin(angles)
    return table.reshape(2 * PADDED, GRID)


def brick_table():
    device = np.arange(COUNT)
    a, b = device // N_PY, device % N_PY
    angles = turn(4 * a[:, None] * a[None, :] + b[:, None] * b[None, :], N_PY)
    return np.concatenate([np.cos(angles), -np.sin(angles)])


def twiddle_tables():
    device = np.arange(COUNT)
    a, b = device // N_PY, device % N_PY
    y, x = CELL_Y, CELL_X
    angles = turn(a[:, None] * x[None, :] + b[:, None] * y[None, :], GRID)
    cosines, sines = np.cos(angles), -np.sin(angles)
    return chunked(cosines, cosines), chunked(-sines, sines)


def cell_table():
    y, x = CELL_Y, CELL_X
    angles = turn(4 * y[:, None] * y[None, :] + x[:, None] * x[None, :], WIDE_X)
    cosines, sines = np.cos(angles), -np.sin(angles)
    table = np.zeros((CHUNKS, 2, HALF, CHUNKS, 2, HALF))
    shape = (CHUNKS, HALF, CHUNKS, HALF)
    table[:, 0, :, :, 0, :] = cosines.reshape(shape)
    table[:, 0, :, :, 1, :] = sines.reshape(shape)
    table[:, 1, :, :, 0, :] = -sines.reshape(shape)
    table[:, 1, :, :, 1, :] = cosines.reshape(shape)
    return table.reshape(2 * CELLS, 2 * CELLS)


def axis_terms(indices):
    signed = np.where(indices <= GRID // 2, indices, indices - GRID) / GRID
    values = [1.0, 0.0]
    for k in range(2, ORDER):
        values = [
            ((k - j) * (values[j - 1] if j >= 1 else 0.0) + (1.0 + j) * (values[j] if j < k else 0.0)) / k
            for j in range(k + 1)
        ]
    total = sum(values[j] * np.exp(1j * turn(indices * j, GRID)) for j in range(ORDER - 1))
    return signed * signed, 1.0 / np.abs(total) ** 2


def green_tables():
    device = np.arange(COUNT)
    freq_x = (device // N_PY)[:, None] + N_PX * CELL_X[None, :]
    freq_y = (device % N_PY)[:, None] + N_PY * CELL_Y[None, :]
    square_x, modulus_x = axis_terms(freq_x)
    square_y, modulus_y = axis_terms(freq_y)
    squares = square_x + square_y
    rate = math.pi * math.pi / (SPLITTING * SPLITTING)
    gains = np.exp(-rate * squares) * modulus_x * modulus_y
    square_z, modulus_z = axis_terms(np.arange(LINES))
    weight = np.full(LINES, 2.0)
    weight[0] = weight[-1] = 1.0
    factor = COUPLING / float(GRID) ** 3
    line = np.zeros((ROWS, 2, LANES))
    line[:LINES, 0] = square_z[:, None]
    line[:LINES, 1] = (factor * weight * np.exp(-rate * square_z) * modulus_z)[:, None]
    return chunked(squares, squares), chunked(gains, -gains), line.reshape(ROWS, 2 * LANES)


def split(value):
    high = value.astype(jnp.bfloat16)
    return high, (value - high.astype(jnp.float32)).astype(jnp.bfloat16)


def product(left, right, dims):
    def one(a, b):
        return lax.dot_general(a, b, dims, preferred_element_type=jnp.float32)

    rows = left[0].shape[0]
    both = one(jnp.concatenate([left[0], left[1]], axis=0), right[0])
    return both[:rows] + both[rows:] + one(left[0], right[1])


def spline_rows(fraction):
    values = [1.0 - fraction, fraction]
    previous = values
    for k in range(2, ORDER):
        previous = values
        updated = []
        for j in range(k + 1):
            terms = []
            if j >= 1:
                terms.append((fraction + float(k - j)) * previous[j - 1])
            if j < k:
                terms.append((float(1 + j) - fraction) * previous[j])
            updated.append(sum(terms[1:], terms[0]) * (1.0 / k))
        values = updated
    slopes = []
    for j in range(ORDER):
        if j == 0:
            slopes.append(-previous[0])
        elif j == ORDER - 1:
            slopes.append(previous[j - 1])
        else:
            slopes.append(previous[j - 1] - previous[j])
    return values, slopes


def place(offset, rows):
    total = jnp.zeros(offset.shape, jnp.float32)
    for j in range(ORDER):
        total = jnp.where(offset == j, rows[j], total)
    return total


def runs_of(number, second):
    size_x, size_y = CLASSES[number][2:]
    found = []
    for (y, begin, end), at in RUNS:
        if (at >= 2 * CELLS // 3) == second and y < size_y and begin < size_x:
            found.append((y, begin, min(end, size_x), at))
    return found


def swap(value):
    return pltpu.roll(value, HALF, 1)


def hand_over(result, potentials, forces):
    potentials[...] = result[0]
    forces[...] = result[1:4]


def kernel(
    charges_any,
    cells_any,
    fractions_any,
    filled_any,
    line_hi_any,
    line_lo_any,
    brick_hi_any,
    brick_lo_any,
    cell_hi_any,
    cell_lo_any,
    twiddle_any,
    green_any,
    line_green_any,
    result,
    charges,
    cells,
    fractions,
    filled,
    line_green,
    line_hi,
    line_lo,
    brick_hi,
    brick_lo,
    cell_hi,
    cell_lo,
    twiddle,
    green,
    atoms,
    wx,
    sx,
    wy,
    sy,
    wz_hi,
    wz_lo,
    column_hi,
    column_lo,
    grid,
    outbound,
    inbound,
    multiplier,
    first_hi,
    first_lo,
    second_hi,
    second_lo,
    returning,
    returned,
    turned_hi,
    turned_lo,
    field_hi,
    field_lo,
    spectrum,
    taps_hi,
    taps_lo,
    offsets,
    sampled,
    partials,
    received,
    table_sems,
    atom_send,
    atom_recv,
    out_send,
    out_recv,
    back_send,
    back_recv,
    part_send,
    part_recv,
    vouched,
):
    px = lax.axis_index("px")
    py = lax.axis_index("py")
    me = px * N_PY + py

    arguments = [
        pltpu.make_async_copy(source, target, table_sems.at[9 + number])
        for number, (source, target) in enumerate(
            [(charges_any, charges), (cells_any, cells), (fractions_any, fractions), (filled_any, filled)]
        )
    ]
    for copy in arguments:
        copy.start()

    barrier = pltpu.get_barrier_semaphore()

    def greet(target):
        pl.semaphore_signal(barrier, inc=1, device_id=target, device_id_type=MESH)

    def greet_row(step, carry):
        greet((px, lax.rem(py + step, N_PY)))
        return carry

    def greet_column(step, carry):
        greet((lax.rem(px + step, N_PX), py))
        return carry

    greet((lax.rem(px + 1, N_PX), lax.rem(py + 1, N_PY)))
    greet((lax.rem(px + N_PX - 1, N_PX), lax.rem(py + N_PY - 1, N_PY)))
    lax.fori_loop(1, N_PX, greet_column, 0)
    lax.fori_loop(1, N_PY, greet_row, 0)

    tables = [
        pltpu.make_async_copy(source, target, table_sems.at[number])
        for number, (source, target) in enumerate(
            [
                (line_hi_any, line_hi),
                (line_lo_any, line_lo),
                (brick_hi_any, brick_hi),
                (brick_lo_any, brick_lo),
                (twiddle_any, twiddle),
                (green_any, green),
                (cell_hi_any, cell_hi),
                (cell_lo_any, cell_lo),
                (line_green_any, line_green),
            ]
        )
    ]
    for table in tables:
        table.start()
    for copy in arguments:
        copy.wait()

    slot = lax.broadcasted_iota(jnp.int32, (1, SLOTS), 1)
    occupied = (slot < filled[...]).astype(jnp.float32)
    weighted = charges[0] * occupied
    atoms[0, 0:1] = weighted
    for d in range(3):
        atoms[0, 1 + d : 2 + d] = cells[d, 0].astype(jnp.float32)
        atoms[0, 4 + d : 5 + d] = fractions[d, 0]
    atoms[0, 7:8] = jnp.zeros((1, SLOTS), jnp.float32)
    returned[:, LINES - 1 :, :] = jnp.zeros((CHUNKS, PADDED - LINES + 1, LANES), jnp.float32)

    def side_tables(number):
        step_x, step_y, size_x, size_y = CLASSES[number]
        values, slopes = spline_rows(atoms[number, 4:7])
        depth_rows(number, values, slopes)
        for row, step, wide, size, weights, rises in (
            (0, step_x, WIDE_X, size_x, wx, sx),
            (1, step_y, WIDE_Y, 16, wy, sy),
        ):
            start = atoms[number, 1 + row : 2 + row].astype(jnp.int32) - step * wide
            offset = lax.broadcasted_iota(jnp.int32, (size, SLOTS), 0) - start
            weights[number, :size] = place(offset, [v[row : row + 1] for v in values])
            rises[number, :size] = place(offset, [v[row : row + 1] for v in slopes])

    def depth_rows(number, values, slopes):
        for kind, rows in enumerate((values, slopes)):
            for j in range(ORDER):
                high, low = split(jnp.broadcast_to(rows[j][2:3], (16, SLOTS)))
                taps_hi[number, kind, j] = high
                taps_lo[number, kind, j] = low
        start = atoms[number, 3:4].astype(jnp.int32)
        offsets[number] = (lax.broadcasted_iota(jnp.int32, (16, SLOTS), 0) - start).astype(jnp.int16)

    def depth_block(number, kind, at, lanes):
        offset = offsets[number] + jnp.full((16, SLOTS), at, jnp.int32).astype(jnp.int16)
        offset = jnp.where(offset < 0, offset + jnp.int16(GRID), offset)
        high = jnp.zeros((16, SLOTS), jnp.bfloat16)
        low = high
        for j in range(ORDER):
            here = offset == j
            high = jnp.where(here, taps_hi[number, kind, j], high)
            low = jnp.where(here, taps_lo[number, kind, j], low)
        wz_hi[pl.ds(at, 16), lanes] = high
        wz_lo[pl.ds(at, 16), lanes] = low

    def depth_tables(number):
        def block(step, carry):
            depth_block(number, 0, pl.multiple_of(step * 16, 16), pl.ds(2 * number * SLOTS, SLOTS))
            return carry

        lax.fori_loop(0, GRID // 16, block, 0)

    def slope_block(step):
        step = jnp.minimum(step, 4 * GRID // 32 - 1)
        number = lax.div(step, GRID // 32)
        at = lax.rem(step, GRID // 32) * 32
        lanes = pl.ds(pl.multiple_of((2 * number + 1) * SLOTS, SLOTS), SLOTS)
        for k in range(2):
            depth_block(number, 1, pl.multiple_of(at + 16 * k, 16), lanes)

    def spread(number, second):
        charge = atoms[number, 0:1]
        total = 0
        for y, begin, end, _ in runs_of(number, second):
            high, low = split((wx[number, begin:end] * charge) * wy[number, y : y + 1])
            column_hi[total : total + end - begin] = high
            column_lo[total : total + end - begin] = low
            total += end - begin
        lanes = pl.ds(2 * number * SLOTS, SLOTS)
        return product((column_hi[:total], column_lo[:total]), (wz_hi[:, lanes], wz_lo[:, lanes]), NT)

    pl.semaphore_wait(barrier, N_PX + N_PY)

    atom_copies = []
    for number in range(1, 4):
        step_x, step_y = CLASSES[number][:2]
        target = (lax.rem(px + step_x, N_PX), lax.rem(py + step_y, N_PY))
        copy = pltpu.make_async_remote_copy(
            atoms.at[0], atoms.at[number], atom_send.at[number], atom_recv.at[number], device_id=target, device_id_type=MESH
        )
        copy.start()
        atom_copies.append(copy)

    def vouch(step, carry):
        pl.semaphore_signal(vouched, inc=1, device_id=(lax.rem(px + step, N_PX), py), device_id_type=MESH)
        return carry

    lax.fori_loop(1, N_PX, vouch, 0)

    side_tables(0)
    depth_tables(0)

    def spread_near(number):
        added = spread(number, False)
        place_at = 0
        for _, begin, end, at in runs_of(number, False):
            grid[at : at + end - begin] += added[place_at : place_at + end - begin]
            place_at += end - begin

    def transform(begin, end):
        lanes = end - begin + (end - begin) % 2
        dense = split(grid[begin * HALF : (begin + lanes) * HALF])
        cosine_part = product((line_hi[:ROWS], line_lo[:ROWS]), dense, NT)
        sine_part = product((line_hi[PADDED : PADDED + ROWS], line_lo[PADDED : PADDED + ROWS]), dense, NT)
        lower = lax.broadcasted_iota(jnp.int32, (ROWS, LANES), 1) < HALF
        for j in range(begin, end):
            at = ((j - begin) // 2) * LANES
            cosine_block = cosine_part[:, at : at + LANES]
            sine_block = sine_part[:, at : at + LANES]
            if (j - begin) % 2 == 0:
                outbound[j] = jnp.where(lower, cosine_block, swap(sine_block))
            else:
                outbound[j] = jnp.where(lower, swap(cosine_block), sine_block)

    first, second = GROUPS
    grid[: first[1] * HALF] = spread(0, False)
    grid[CELLS:] = jnp.zeros((HALF, GRID), jnp.float32)
    for number in range(1, 4):
        atom_copies[number - 1].wait_recv()
        side_tables(number)
        depth_tables(number)
        spread_near(number)
    tables[0].wait()
    tables[1].wait()
    transform(*first)
    pl.semaphore_wait(vouched, N_PX - 1)

    core_me = lax.rem(px, 2)
    low_me = lax.div(px, 2)
    z_me = 4 * lax.div(py, 16) + low_me
    x_me = lax.rem(lax.div(py, 4), 4)
    y_me = lax.rem(py, 4)

    def main_core(low, to_y):
        return lax.rem(low + lax.div(to_y, 8) + lax.div(lax.rem(to_y, 4), 2), 2)

    order = low_me * N_PY + py
    main_me = main_core(low_me, py)
    other_me = lax.rem(core_me + main_me, 2)
    last = jnp.logical_and(px == 1, py == 1)
    matching = jnp.logical_and(other_me == 1, lax.rem(low_me + x_me + y_me, 2) == 0)
    active = jnp.logical_or(jnp.logical_or(other_me == 0, last), matching)
    line_me = (1 - other_me) * order + other_me * (128 + lax.div(order, 2))
    line_me = line_me + last.astype(jnp.int32) * (LINES - 1 - 128)

    def part(buffer, group, row):
        begin, end = GROUPS[group][:2]
        return buffer.at[pl.ds(begin, end - begin), pl.ds(row, 1), :]

    def keep_line(group):
        pltpu.make_async_copy(part(outbound, group, line_me), part(inbound, group, me), out_recv.at[group]).start()

    def send_line(group, line, to_x, to_y):
        pltpu.make_async_remote_copy(
            part(outbound, group, line),
            part(inbound, group, me),
            out_send.at[group],
            out_recv.at[group],
            device_id=(to_x, to_y),
            device_id_type=MESH,
        ).start()

    def farthest(middle, phase):
        far = lax.div(phase + 1, 2)
        return middle + (2 * lax.rem(phase, 2) - 1) * -far

    def send_even(group, low, high, x, move_y):
        to_y = 16 * high + 4 * x + lax.rem(y_me + move_y, 4)
        send_line(group, N_PY * low + to_y, 2 * low + main_core(low, to_y), to_y)

    def send_odd(group, low, high, x, move_pair):
        pair = lax.rem(lax.div(y_me, 2) + move_pair, 2)
        to_y = 16 * high + 4 * x + 2 * pair + lax.rem(low + x, 2)
        line = 128 + 16 * low + 8 * high + 2 * x + pair
        send_line(group, line, 2 * low + 1 - main_core(low, to_y), to_y)

    def send_group(group):
        def send_column(move_z, move_x, skip=0):
            z = lax.rem(z_me + move_z, 8)
            low, high = lax.rem(z, 4), lax.div(z, 4)
            x = lax.rem(x_me + move_x, 4)
            for k in [far for far in (2, 1, 3, 0) if far >= skip]:
                send_even(group, low, high, x, k)
            for k in range(min(skip, 1), 2):
                send_odd(group, low, high, x, k)

        def send_far(step, carry):
            send_column(farthest(4, lax.div(step, 4)), farthest(2, lax.rem(step, 4)))
            slope_block(28 * group + step)
            return carry

        def send_near(step, carry):
            send_column(0, step)
            return carry

        lax.fori_loop(0, 28, send_far, 0)
        lax.fori_loop(1, 4, send_near, 0)
        send_column(0, 0, skip=1)
        high = lax.div(py, 16)
        pl.when(active)(lambda: keep_line(group))
        pl.when(other_me == 1)(lambda: send_even(group, low_me, high, x_me, 0))
        pl.when(jnp.logical_not(matching))(lambda: send_odd(group, low_me, high, x_me, 0))
        pl.when(jnp.logical_not(last))(lambda: send_line(group, LINES - 1, 1, 1))

    send_group(0)
    grid[second[0] * HALF : CELLS] = spread(0, True)
    transform(*second)
    send_group(1)

    for table in tables[2:]:
        table.wait()

    def wait_rows(buffer, group, count, semaphores):
        begin, end = GROUPS[group][:2]
        view = buffer.at[pl.ds(begin, end - begin), pl.ds(0, count), :]
        pltpu.make_async_copy(view, view, semaphores.at[group]).wait()

    @pl.when(active)
    def _():
        left = lax.broadcasted_iota(jnp.int32, (COUNT, LANES), 1) < HALF
        brick_pair = (brick_hi[...], brick_lo[...])

        def pairs(group):
            begin, end = GROUPS[group][:2]
            return [(j, min(j + 2, end)) for j in range(begin, end, 2)]

        def turned(value, j):
            return value * twiddle[0, j] + swap(value) * twiddle[1, j]

        def gather(group):
            for begin, end in pairs(group):
                block = jnp.concatenate([inbound[j] for j in range(begin, end)], axis=1)
                mixed = product(brick_pair, split(block), NN)
                for j in range(begin, end):
                    at = (j - begin) * LANES
                    upper = mixed[:COUNT, at : at + LANES]
                    crossed = swap(mixed[COUNT:, at : at + LANES])
                    value = upper + jnp.where(left, -crossed, crossed)
                    high, low = split(turned(value, j))
                    first_hi[:, j * LANES : (j + 1) * LANES] = high
                    first_lo[:, j * LANES : (j + 1) * LANES] = low

        def over_cells(group, lanes):
            rows = slice(GROUPS[group][0] * LANES, GROUPS[group][1] * LANES)
            return product((first_hi[:, rows], first_lo[:, rows]), (cell_hi[rows, lanes], cell_lo[rows, lanes]), NN)

        every = pairs(0) + pairs(1)
        wait_rows(inbound, 0, COUNT, out_recv)
        gather(0)
        for begin, end in every:
            lanes = slice(begin * LANES, end * LANES)
            spectrum[:, lanes] = over_cells(0, lanes)

        scalars = line_green[pl.ds(line_me, 1), :]
        square_z = scalars[:, :LANES]
        gain_z = scalars[:, LANES:]
        for j in range(CHUNKS):
            squared = green[0, j] + square_z
            positive = squared > 0.0
            bounded = jnp.where(positive, squared, 1.0)
            multiplier[j] = jnp.where(positive, green[1, j] * gain_z / bounded, 0.0)

        wait_rows(inbound, 1, COUNT, out_recv)
        gather(1)
        for begin, end in every:
            lanes = slice(begin * LANES, end * LANES)
            block = spectrum[:, lanes] + over_cells(1, lanes)
            for j in range(begin, end):
                at = (j - begin) * LANES
                high, low = split(block[:, at : at + LANES] * multiplier[j])
                second_hi[:, j * LANES : (j + 1) * LANES] = high
                second_lo[:, j * LANES : (j + 1) * LANES] = low

        def send_row(group, to_x, to_y):
            other = N_PY * to_x + to_y
            pltpu.make_async_remote_copy(
                part(returning, group, other),
                part(returned, group, line_me),
                back_send.at[group],
                back_recv.at[group],
                device_id=(to_x, to_y),
                device_id_type=MESH,
            ).start()

        def send_rows(group, move_core, move_z, move_x, skip=0):
            z = lax.rem(z_me + move_z, 8)
            to_x = 2 * lax.rem(z, 4) + lax.rem(core_me + move_core, 2)
            base = 16 * lax.div(z, 4) + 4 * lax.rem(x_me + move_x, 4)
            for k in [far for far in (2, 1, 3, 0) if far >= skip]:
                send_row(group, to_x, base + lax.rem(y_me + k, 4))

        for group in range(2):
            for begin, end in pairs(group):
                lanes = slice(begin * LANES, end * LANES)
                block = product((second_hi[...], second_lo[...]), (cell_hi[:, lanes], cell_lo[:, lanes]), NN)
                block = jnp.concatenate(
                    [turned(block[:, (j - begin) * LANES : (j - begin + 1) * LANES], j) for j in range(begin, end)], axis=1
                )
                mixed = product(brick_pair, split(block), NN)
                for j in range(begin, end):
                    at = (j - begin) * LANES
                    upper = mixed[:COUNT, at : at + LANES]
                    crossed = swap(mixed[COUNT:, at : at + LANES])
                    returning[j] = jnp.where(left, upper, -upper) - crossed

            def send_far(step, carry, group=group):
                phase = lax.div(step, 8)
                send_rows(group, lax.rem(lax.div(step, 4), 2), farthest(4, phase), farthest(2, lax.rem(step, 4)))
                return carry

            def send_near(step, carry, group=group):
                send_rows(group, lax.div(step, 4), 0, lax.rem(step, 4))
                return carry

            lax.fori_loop(0, 56, send_far, 0)
            lax.fori_loop(1, 8, send_near, 0)
            send_rows(group, 0, 0, 0, skip=1)
            pltpu.make_async_copy(part(returning, group, me), part(returned, group, line_me), back_recv.at[group]).start()

    def restore(group):
        begin, end = GROUPS[group][:2]
        wait_rows(returned, group, LINES, back_recv)
        for j in range(begin, end):
            high, low = split(returned[j].T)
            rows = slice(j * HALF, (j + 1) * HALF)
            turned_hi[rows, :PADDED] = high[:HALF]
            turned_hi[rows, PADDED:] = high[HALF:]
            turned_lo[rows, :PADDED] = low[:HALF]
            turned_lo[rows, PADDED:] = low[HALF:]
        rows = slice(begin * HALF, end * HALF)
        high, low = split(product((turned_hi[rows], turned_lo[rows]), (line_hi[...], line_lo[...]), NN))
        field_hi[rows] = high
        field_lo[rows] = low

    def sample(number, second):
        runs = runs_of(number, second)
        total = sum(end - begin for _, begin, end, _ in runs)
        if number < 2:
            first_at = runs[0][3]
            field = (field_hi[first_at : first_at + total], field_lo[first_at : first_at + total])
        else:
            field = tuple(
                jnp.concatenate([values[at : at + end - begin] for _, begin, end, at in runs], axis=0)
                for values in (field_hi, field_lo)
            )
        lanes = slice(2 * number * SLOTS, 2 * (number + 1) * SLOTS)
        sampled[:total] = product(field, (wz_hi[:, lanes], wz_lo[:, lanes]), NN)

        def block(step, carry):
            at = pl.multiple_of(step * LANES, LANES)
            here = pl.ds(at, LANES)
            found = {}
            row_at = 0
            for y, begin, end, _ in runs:
                rows = slice(row_at, row_at + end - begin)
                row_at += end - begin
                level = sampled[rows, here]
                rising = sampled[rows, pl.ds(SLOTS + at, LANES)]
                weight = wy[number, y : y + 1, here]
                terms = [weight * level, sy[number, y : y + 1, here] * level, weight * rising]
                before = found.get((begin, end))
                found[begin, end] = terms if before is None else [a + b for a, b in zip(before, terms)]
            sums = None
            for (begin, end), (over_y, slope_over_y, rising_over_y) in found.items():
                weight = wx[number, begin:end, here]
                terms = [weight * over_y, sx[number, begin:end, here] * over_y]
                terms += [weight * slope_over_y, weight * rising_over_y]
                terms = [jnp.sum(values, axis=0, keepdims=True) for values in terms]
                sums = terms if sums is None else [a + b for a, b in zip(sums, terms)]
            for row, total_row in enumerate(sums):
                if second:
                    total_row = total_row + partials[number, row : row + 1, here]
                partials[number, row : row + 1, here] = total_row
            return carry

        lax.fori_loop(0, SLOTS // LANES, block, 0)

    part_copies = []

    def give(number):
        step_x, step_y = CLASSES[number][:2]
        target = (lax.rem(px + N_PX - step_x, N_PX), lax.rem(py + N_PY - step_y, N_PY))
        copy = pltpu.make_async_remote_copy(
            partials.at[number],
            received.at[number],
            part_send.at[number],
            part_recv.at[number],
            device_id=target,
            device_id_type=MESH,
        )
        copy.start()
        part_copies.append(copy)

    restore(0)
    for number in range(1, 4):
        sample(number, False)
        give(number)
    sample(0, False)
    restore(1)
    sample(0, True)
    summed = partials[0, 0:4]
    for copy in part_copies:
        copy.wait_recv()
    for number in range(1, 4):
        summed = summed + received[number, 0:4]
    result[0, 0] = summed[0:1] * occupied
    for d in range(3):
        result[1 + d, 0] = -weighted * summed[1 + d : 2 + d]

    for copy in atom_copies + part_copies:
        copy.wait_send()

    @pl.when(active)
    def _():
        for group in range(2):
            wait_rows(outbound, group, LINES - 1, out_send)
            wait_rows(returning, group, COUNT - 1, back_send)

    @pl.when(jnp.logical_not(active))
    def _():
        for group in range(2):
            wait_rows(outbound, group, LINES, out_send)


def shards(charges, cells, fractions, filled):
    line = halves(line_table())
    brick = halves(brick_table())
    cell = halves(cell_table())
    twiddle = np.stack(twiddle_tables()).astype(np.float32)
    squares, gains, line_green = green_tables()
    green = np.stack([squares, gains]).astype(np.float32)
    constants = [*line, *brick, *cell, twiddle, green, line_green.astype(np.float32)]
    f32, bf16 = jnp.float32, jnp.bfloat16
    vmem = pltpu.VMEM
    message = vmem((CHUNKS, COUNT, LANES), f32)
    plane = vmem((COUNT, 2 * CELLS), bf16)
    whole = pl.BlockSpec(memory_space=pltpu.VMEM)
    distant = pl.BlockSpec(memory_space=pl.ANY)
    result = pl.pallas_call(
        kernel,
        out_shape=jax.ShapeDtypeStruct((4, 1, 1, SLOTS), f32),
        in_specs=[distant] * 13,
        out_specs=whole,
        scratch_shapes=[
            vmem((1, 1, SLOTS), f32),
            vmem((3, 1, 1, SLOTS), jnp.int32),
            vmem((3, 1, 1, SLOTS), f32),
            vmem((1, 1), jnp.int32),
            vmem((ROWS, 2 * LANES), f32),
            vmem((2 * PADDED, GRID), bf16),
            vmem((2 * PADDED, GRID), bf16),
            vmem((2 * COUNT, COUNT), bf16),
            vmem((2 * COUNT, COUNT), bf16),
            vmem((2 * CELLS, 2 * CELLS), bf16),
            vmem((2 * CELLS, 2 * CELLS), bf16),
            vmem((2, CHUNKS, COUNT, LANES), f32),
            vmem((2, CHUNKS, COUNT, LANES), f32),
            vmem((4, 8, SLOTS), f32),
            vmem((4, WIDE_X, SLOTS), f32),
            vmem((4, WIDE_X, SLOTS), f32),
            vmem((4, 16, SLOTS), f32),
            vmem((4, 16, SLOTS), f32),
            vmem((GRID, 8 * SLOTS), bf16),
            vmem((GRID, 8 * SLOTS), bf16),
            vmem((CELLS, SLOTS), bf16),
            vmem((CELLS, SLOTS), bf16),
            vmem((CELLS + HALF, GRID), f32),
            vmem((CHUNKS, ROWS, LANES), f32),
            message,
            message,
            plane,
            plane,
            plane,
            plane,
            message,
            message,
            vmem((CELLS, 2 * PADDED), bf16),
            vmem((CELLS, 2 * PADDED), bf16),
            vmem((CELLS, GRID), bf16),
            vmem((CELLS, GRID), bf16),
            vmem((COUNT, 2 * CELLS), f32),
            vmem((4, 2, ORDER, 16, SLOTS), bf16),
            vmem((4, 2, ORDER, 16, SLOTS), bf16),
            vmem((4, 16, SLOTS), jnp.int16),
            vmem((CELLS, 2 * SLOTS), f32),
            vmem((4, 8, SLOTS), f32),
            vmem((4, 8, SLOTS), f32),
            pltpu.SemaphoreType.DMA((13,)),
            pltpu.SemaphoreType.DMA((4,)),
            pltpu.SemaphoreType.DMA((4,)),
            pltpu.SemaphoreType.DMA((2,)),
            pltpu.SemaphoreType.DMA((2,)),
            pltpu.SemaphoreType.DMA((2,)),
            pltpu.SemaphoreType.DMA((2,)),
            pltpu.SemaphoreType.DMA((4,)),
            pltpu.SemaphoreType.DMA((4,)),
            pltpu.SemaphoreType.REGULAR,
        ],
        compiler_params=pltpu.CompilerParams(
            collective_id=0, has_side_effects=True, vmem_limit_bytes=56 * 1024 * 1024
        ),
    )(charges, cells, fractions, filled, *[jnp.asarray(table) for table in constants])
    return pl.pallas_call(
        hand_over,
        out_shape=(jax.ShapeDtypeStruct((1, 1, SLOTS), f32), jax.ShapeDtypeStruct((3, 1, 1, SLOTS), f32)),
        in_specs=[whole],
        out_specs=(whole, whole),
    )(result)


def solution(mesh):
    placed = (
        P("px", "py", None),
        P(None, "px", "py", None),
        P(None, "px", "py", None),
        P("px", "py"),
    )
    return jax.shard_map(
        shards,
        mesh=mesh,
        in_specs=placed,
        out_specs=(P("px", "py", None), P(None, "px", "py", None)),
        check_vma=False,
    )
```
